256 devices in a mesh: row: 16 (over x, y), col: 16 (over z, core).
Axes of the slice: x: 4, y: 4, z: 8, core: 2. Of those that a mesh axis runs over, the one named last changes fastest.
Arguments:
- activations: bfloat16 [8192, 2048], P('row'), may hold values from -6 to 6
- cotangent: bfloat16 [8192, 2048], P('row'), may hold values from -6 to 6
- router: float32 [2048, 16], replicated, may hold values from -3 to 3
- gate_experts: bfloat16 [16, 2048, 5632], P(None, 'row', 'col'), may hold values from -0.125 to 0.125
- up_experts: bfloat16 [16, 2048, 5632], P(None, 'row', 'col'), may hold values from -0.125 to 0.125
- down_experts: bfloat16 [16, 5632, 2048], P(None, 'col', 'row'), may hold values from -0.078125 to 0.078125
- route_source: int32 [32], replicated, may hold values from 0 to 30, as said below
Outputs:
- input_grad: bfloat16 [8192, 2048], P('row')
- gate_grad: bfloat16 [16, 2048, 5632], P(None, 'row', 'col')
- up_grad: bfloat16 [16, 2048, 5632], P(None, 'row', 'col')
- down_grad: bfloat16 [16, 5632, 2048], P(None, 'col', 'row')
- router_grad: float32 [2048, 16], replicated
The draws below stay inside these ranges and needn't reach their ends.
Inputs may be any that keep to these rules, and one draw needn't show every extreme that they name: route_source[0] = 0, and for every later segment s it names s - 1 or s - 2 (never below 0); the last segment names 30.
All inputs are finite; a program needn't handle non-finite values.
Results may differ from the reference program's by a relative error of at most 0.011.
Values may be sent and summed in bfloat16 or wider, within the bound.
A program may use at most 128 MiB of HBM per device.

```python
import jax
import jax.numpy as jnp
from jax import lax

E = 16
D = 2048
FF = 5632
SEG_LEN = 256
SEGS = 32
TOKENS = 8192


def draw_route_source(key, part):
    key = jax.random.fold_in(key, 7)
    delays = jax.random.randint(key, (SEGS,), 1, 3)
    places = jnp.arange(SEGS, dtype=jnp.int32)
    sources = jnp.maximum(places - delays, 0)
    sources = jnp.where(places == SEGS - 1, SEGS - 2, sources)
    return sources.astype(jnp.int32)


def steps_of(key, shape, shards, least, largest):
    level = 1.0
    for position, blocks in shards:
        draws = jax.random.uniform(jax.random.fold_in(jax.random.fold_in(key, 6), position), (blocks,), jnp.float32, least / len(shards), largest / len(shards))
        level = level * jnp.repeat(jnp.exp(draws), shape[position] // blocks).reshape((-1,) + (1,) * (len(shape) - 1 - position))
    return level


def noise(stream_key, shape, width, most, cuts=(), kind=jnp.bfloat16):
    level = steps_of(stream_key, shape, cuts, -0.22, 0.18) if cuts else 1.0
    values = jax.random.normal(stream_key, shape, jnp.float32) * width * level
    return jnp.minimum(jnp.maximum(values, -most), most).astype(kind)


def setup_inputs(seed: int = 0) -> dict:
    keys = jax.random.split(jax.random.key(seed), 8)
    activations = noise(keys[0], (TOKENS, D), 1.0, 6.0, ((0, 16),))
    cotangent = noise(keys[1], (TOKENS, D), 1.0, 6.0, ((0, 16),))
    router = noise(keys[2], (D, E), 0.5, 3.0, (), jnp.float32)
    gate_experts = noise(keys[3], (E, D, FF), D ** -0.5, 0.125, ((1, 16), (2, 16)))
    up_experts = noise(keys[4], (E, D, FF), D ** -0.5, 0.125, ((1, 16), (2, 16)))
    down_experts = noise(keys[5], (E, FF, D), FF ** -0.5, 0.078125, ((1, 16), (2, 16)))
    route_source = draw_route_source(jax.random.fold_in(keys[7], 71), 0)
    return dict(activations=activations, cotangent=cotangent, router=router, gate_experts=gate_experts, up_experts=up_experts, down_experts=down_experts, route_source=route_source)


PRECISE = lax.Precision.HIGHEST


def reference(activations, cotangent, router, gate_experts, up_experts, down_experts, route_source):
    means = jnp.mean(activations.reshape(SEGS, SEG_LEN, D), axis=1, dtype=jnp.float32)
    scores = jnp.dot(means, router, precision=PRECISE)
    chooser = (route_source[:, None] == jnp.arange(SEGS, dtype=jnp.int32)[None, :]).astype(jnp.float32)
    logits = jnp.dot(chooser, scores, precision=PRECISE)
    powers = jnp.exp(logits)
    routes = powers / jnp.sum(powers, axis=-1, keepdims=True)
    rounded = routes.astype(jnp.bfloat16)
    gate_flat = gate_experts.reshape(E, D * FF)
    up_flat = up_experts.reshape(E, D * FF)
    down_flat = down_experts.reshape(E, FF * D)

    def segment(index):
        tokens = lax.dynamic_slice_in_dim(activations, index * SEG_LEN, SEG_LEN, 0)
        output_gradients = lax.dynamic_slice_in_dim(cotangent, index * SEG_LEN, SEG_LEN, 0)
        weights = rounded[index]
        combined_gate_weight = jnp.dot(weights, gate_flat, preferred_element_type=jnp.float32).astype(jnp.bfloat16).reshape(D, FF)
        combined_up_weight = jnp.dot(weights, up_flat, preferred_element_type=jnp.float32).astype(jnp.bfloat16).reshape(D, FF)
        combined_down_weight = jnp.dot(weights, down_flat, preferred_element_type=jnp.float32).astype(jnp.bfloat16).reshape(FF, D)
        gate_preactivation = jnp.dot(tokens, combined_gate_weight, preferred_element_type=jnp.float32)
        up_preactivation = jnp.dot(tokens, combined_up_weight, preferred_element_type=jnp.float32)
        sigmoid_gate = jax.nn.sigmoid(gate_preactivation)
        gate_act = gate_preactivation * sigmoid_gate
        hidden_state = (gate_act * up_preactivation).astype(jnp.bfloat16)
        hidden_grad = jnp.dot(output_gradients, combined_down_weight.T, preferred_element_type=jnp.float32)
        gate_difference = (hidden_grad * up_preactivation * sigmoid_gate * (1.0 + gate_preactivation * (1.0 - sigmoid_gate))).astype(jnp.bfloat16)
        up_difference = (hidden_grad * gate_act).astype(jnp.bfloat16)
        gate_terms = jnp.dot(tokens.T, gate_difference, preferred_element_type=jnp.float32).astype(jnp.bfloat16)
        up_terms = jnp.dot(tokens.T, up_difference, preferred_element_type=jnp.float32).astype(jnp.bfloat16)
        down_terms = jnp.dot(hidden_state.T, output_gradients, preferred_element_type=jnp.float32).astype(jnp.bfloat16)
        direct_grad = jnp.dot(gate_difference, combined_gate_weight.T, preferred_element_type=jnp.float32)
        direct_grad = direct_grad + jnp.dot(up_difference, combined_up_weight.T, preferred_element_type=jnp.float32)
        route_part = jnp.dot(gate_flat, gate_terms.reshape(-1), preferred_element_type=jnp.float32)
        route_part = route_part + jnp.dot(up_flat, up_terms.reshape(-1), preferred_element_type=jnp.float32)
        route_part = route_part + jnp.dot(down_flat, down_terms.reshape(-1), preferred_element_type=jnp.float32)
        return direct_grad, gate_terms.reshape(-1), up_terms.reshape(-1), down_terms.reshape(-1), route_part

    direct_grad, gate_terms, up_terms, down_terms, route_grad = lax.map(segment, jnp.arange(SEGS, dtype=jnp.int32))
    logit_grad = routes * (route_grad - jnp.sum(routes * route_grad, axis=-1, keepdims=True))
    source_grad = jnp.dot(chooser.T, logit_grad, precision=PRECISE)
    router_grad = jnp.dot(means.T, source_grad, precision=PRECISE)
    mean_grad = jnp.dot(source_grad, router.T, precision=PRECISE)
    input_grad = (direct_grad + mean_grad[:, None, :] / SEG_LEN).reshape(TOKENS, D).astype(jnp.bfloat16)
    gate_grad = jnp.dot(rounded.T, gate_terms, preferred_element_type=jnp.float32).astype(jnp.bfloat16).reshape(E, D, FF)
    up_grad = jnp.dot(rounded.T, up_terms, preferred_element_type=jnp.float32).astype(jnp.bfloat16).reshape(E, D, FF)
    down_grad = jnp.dot(rounded.T, down_terms, preferred_element_type=jnp.float32).astype(jnp.bfloat16).reshape(E, FF, D)
    return input_grad, gate_grad, up_grad, down_grad, router_grad
```

```python
import functools

import jax
import jax.numpy as jnp
from jax import lax
from jax.experimental import pallas as pl
from jax.experimental.pallas import tpu as pltpu
from jax.sharding import PartitionSpec as P

SEG = 256
EXPERTS = 16
SIDE = 4
DEPTH = 8
BLOCK = 128
HALF = 176
LANES = 3 * BLOCK
WIDE = SIDE * BLOCK
GROUP = 16
CHUNK = 16
PRECISE = lax.Precision.HIGHEST
MESH = pl.DeviceIdType.MESH
F32 = jnp.float32
BF16 = jnp.bfloat16


def dot_nn(a, b):
    return lax.dot_general(a, b, (((1,), (0,)), ((), ())), preferred_element_type=F32)


def dot_nt(a, b):
    return lax.dot_general(a, b, (((1,), (1,)), ((), ())), preferred_element_type=F32)


def dot_tn(a, b):
    return lax.dot_general(a, b, (((0,), (0,)), ((), ())), preferred_element_type=F32)


def drain(ref, sem):
    pltpu.make_async_copy(ref, ref, sem).wait()


def kernel(
    act, cot, gate_t, up_t, down, spread, spread_t,
    gate_out, up_out, down_out, inner_out, direct_out,
    experts, tokens, merged, weights, terms, part_out, part_in, deltas,
    direct, from_pair, to_depth, from_depth, depth_sum, to_owner, direct_all, inner,
    e_sem, tok_sem, tok_send, pass_send, m_send, m_recv, p_send, p_recv, d_send, d_recv,
    t_send, t_recv, s_send, s_recv, z_send, z_recv, o_send, o_recv, a_send, a_recv,
    f_send, f_recv, out_sem,
):
    row = lax.axis_index("row")
    col = lax.axis_index("col")
    x, y = row // SIDE, row % SIDE
    z, k = col // 2, col % 2
    sibling = (row, z * 2 + 1 - k)

    def line(h, at):
        return jnp.where(h == 0, at * SIDE + y, x * SIDE + at)

    def cross(h, at):
        return jnp.where(h == 0, x * SIDE + at, at * SIDE + y)

    def send(src, dst, send_sem, recv_sem, to):
        pltpu.make_async_remote_copy(
            src_ref=src, dst_ref=dst, send_sem=send_sem, recv_sem=recv_sem,
            device_id=to, device_id_type=MESH,
        ).start()

    loads = [
        pltpu.make_async_copy(src, experts.at[:, :, pl.ds(n * BLOCK, BLOCK)], e_sem.at[n])
        for n, src in enumerate((gate_t, up_t, down))
    ]
    for load in loads:
        load.start()

    peers = []
    for o in range(1, SIDE):
        peers.append((((x + o) % SIDE) * SIDE + y, col))
        peers.append((x * SIDE + (y + o) % SIDE, col))
    for o in range(1, DEPTH):
        peers.append((row, ((z + o) % DEPTH) * 2 + k))
    peers.append(sibling)
    barrier = pltpu.get_barrier_semaphore()
    for peer in peers:
        pl.semaphore_signal(barrier, inc=1, device_id=peer, device_id_type=MESH)
    pl.semaphore_wait(barrier, len(peers))

    mine = pl.multiple_of(k * SEG, SEG)
    for o in range(1, SIDE):
        to = (x + o) % SIDE
        for n, src in enumerate((act, cot)):
            send(
                src.at[pl.ds(mine, SEG), pl.ds(pl.multiple_of(to * WIDE, WIDE), WIDE)],
                tokens.at[0, SIDE * k + x, n],
                tok_send.at[0, o - 1], tok_sem.at[0, SIDE * k + x], (to * SIDE + y, col),
            )
        to = (y + o) % SIDE
        for n, src in enumerate((act, cot)):
            for q in range(SIDE):
                send(
                    src.at[pl.ds(mine, SEG), pl.ds(pl.multiple_of((q * SIDE + to) * BLOCK, BLOCK), BLOCK)],
                    tokens.at[1, SIDE * k + y, n, :, pl.ds(q * BLOCK, BLOCK)],
                    tok_send.at[1, o - 1], tok_sem.at[1, SIDE * k + y], (x * SIDE + to, col),
                )
    for b in range(2):
        rows = pl.ds(b * SEG, SEG)
        for n, src in enumerate((act, cot)):
            pltpu.make_async_copy(
                src.at[rows, pl.ds(pl.multiple_of(x * WIDE, WIDE), WIDE)],
                tokens.at[0, SIDE * b + x, n], tok_sem.at[0, SIDE * b + x],
            ).start()
            for q in range(SIDE):
                pltpu.make_async_copy(
                    src.at[rows, pl.ds(pl.multiple_of((q * SIDE + y) * BLOCK, BLOCK), BLOCK)],
                    tokens.at[1, SIDE * b + y, n, :, pl.ds(q * BLOCK, BLOCK)],
                    tok_sem.at[1, SIDE * b + y],
                ).start()
    for load in loads:
        load.wait()

    for b in range(2):
        for h in range(2):

            @pl.loop(0, HALF // GROUP)
            def _(g):
                at = pl.multiple_of(g * GROUP, GROUP)
                chunk = experts[:, pl.ds(h * HALF + at, GROUP), :].reshape(EXPERTS * GROUP, LANES)
                out = dot_nn(spread[b], chunk).astype(BF16)
                merged[h, b, :, pl.ds(at, GROUP), :] = out.reshape(SIDE * SIDE, GROUP, LANES)

            own = x if h == 0 else y
            side = y if h == 0 else x

            @pl.loop(0, SIDE)
            def _(t):
                q = (own + 1 + t) % SIDE
                for o in range(SIDE):
                    to = (side + o) % SIDE
                    slot = q * SIDE + to if h == 0 else to * SIDE + q
                    src = merged.at[h, b, slot]
                    dst = weights.at[h, SIDE * b + q, side]
                    if o == 0:
                        pltpu.make_async_copy(src, dst, m_recv.at[h, SIDE * b + q]).start()
                    else:
                        device = x * SIDE + to if h == 0 else to * SIDE + y
                        send(src, dst, m_send.at[h, b], m_recv.at[h, SIDE * b + q], (device, col))

    for o in range(1, SIDE):
        for h in range(2):
            own = x if h == 0 else y
            j = SIDE * k + (own + o) % SIDE
            drain(tokens.at[h, j], tok_sem.at[h, j])
            send(tokens.at[h, j], tokens.at[h, j], pass_send.at[h, o - 1], tok_sem.at[h, j], sibling)
    for h in range(2):
        own = x if h == 0 else y
        for b in range(2):
            drain(tokens.at[h, SIDE * b + own], tok_sem.at[h, SIDE * b + own])
        for o in range(1, SIDE):
            j = SIDE * (1 - k) + (own + o) % SIDE
            drain(tokens.at[h, j], tok_sem.at[h, j])

    def joined(h, j, n):
        return jnp.concatenate(
            [weights[h, j, q, :, n * BLOCK:(n + 1) * BLOCK] for q in range(SIDE)], axis=1
        )

    @pl.loop(0, 16)
    def _(i):
        b, t, h = i // 8, (i // 2) % SIDE, i % 2
        own = jnp.where(h == 0, x, y)
        q = (own + 1 + t) % SIDE
        j = SIDE * b + q
        drain(weights.at[h, j], m_recv.at[h, j])
        for n in range(3):
            side = tokens[h, j, 0 if n < 2 else 1]
            part_out[h, j, n] = dot_nt(joined(h, j, n), side).astype(BF16)

        @pl.when(t < SIDE - 1)
        def _():
            send(part_out.at[h, j], part_in.at[h, b, t], p_send.at[h, j], p_recv.at[h, b], (line(h, q), col))

    @pl.loop(0, 4)
    def _(i):
        b, h = i // 2, i % 2
        own = jnp.where(h == 0, x, y)
        j = SIDE * b + own
        drain(part_in.at[h, b], p_recv.at[h, b])

        def total(n):
            out = part_out[h, j, n].astype(F32)
            for o in range(SIDE - 1):
                out += part_in[h, b, o, n].astype(F32)
            return out

        gate, up, grad = total(0), total(1), total(2)
        sig = jax.nn.sigmoid(gate)
        gated = gate * sig
        deltas[h, j, 0] = (grad * up * sig * (1.0 + gate * (1.0 - sig))).astype(BF16)
        deltas[h, j, 1] = (grad * gated).astype(BF16)
        deltas[h, j, 2] = (gated * up).astype(BF16)
        for o in range(1, SIDE):
            send(
                deltas.at[h, j], deltas.at[h, j], d_send.at[h, b], d_recv.at[h, j],
                (line(h, (own + o) % SIDE), col),
            )

    def item(i):
        b, t, h = i // 8, (i // 2) % SIDE, i % 2
        own = jnp.where(h == 0, x, y)
        q = (own + t) % SIDE
        return b, t, h, q, SIDE * b + q

    def pair_sum(i):
        b, t, h, q, j = item(i)
        drain(from_pair.at[h, j], s_recv.at[h, j])
        out = direct[i % 4, k].astype(F32) + from_pair[h, j].astype(F32)
        to_depth[h, j] = out.astype(BF16).reshape(DEPTH, CHUNK, WIDE)

        @pl.loop(1, DEPTH)
        def _(o):
            to = (z + o) % DEPTH
            send(
                to_depth.at[h, j, to], from_depth.at[h, j, o - 1], z_send.at[h, j], z_recv.at[h, j],
                (row, to * 2 + k),
            )

    @pl.loop(0, 16)
    def _(i):
        b, t, h, q, j = item(i)

        @pl.when(t > 0)
        def _():
            drain(deltas.at[h, j], d_recv.at[h, j])

        @pl.when(i >= 4)
        def _():
            drain(direct.at[0, 0], s_send.at[i % 4])

        both = deltas[h, j, 0:2].reshape(2 * HALF, SEG)
        out = dot_tn(both, jnp.concatenate([joined(h, j, 0), joined(h, j, 1)], axis=0))
        direct[i % 4] = out.astype(BF16).reshape(2, SEG // 2, WIDE)
        send(direct.at[i % 4, 1 - k], from_pair.at[h, j], s_send.at[i % 4], s_recv.at[h, j], sibling)

        for n in range(3):
            side = tokens[h, j, 0 if n < 2 else 1]
            out = dot_nn(deltas[h, j, n], side).astype(BF16)
            for p in range(SIDE):
                weights[h, j, p, :, n * BLOCK:(n + 1) * BLOCK] = out[:, p * BLOCK:(p + 1) * BLOCK]
        side = jnp.where(h == 0, y, x)
        slot = jnp.where(h == 0, q * SIDE + y, x * SIDE + q)
        for o in range(1, SIDE):
            to = (side + o) % SIDE
            send(
                weights.at[h, j, to], terms.at[h, b, slot], t_send.at[h, j], t_recv.at[h, b],
                (cross(h, to), col),
            )
        pltpu.make_async_copy(weights.at[h, j, side], terms.at[h, b, slot], t_recv.at[h, b]).start()

        @pl.when(i > 0)
        def _():
            pair_sum(i - 1)

    pair_sum(15)

    @pl.loop(0, 16)
    def _(i):
        b, t, h, q, j = item(i)
        drain(from_depth.at[h, j], z_recv.at[h, j])
        out = to_depth[h, j, z].astype(F32)
        for o in range(DEPTH - 1):
            out += from_depth[h, j, o].astype(F32)
        depth_sum[h, j] = out.astype(BF16)
        own = jnp.where(h == 0, x, y)

        @pl.when(t == 0)
        def _():
            to_owner[h, b, own] = out.astype(BF16)

        @pl.when(t > 0)
        def _():
            send(
                depth_sum.at[h, j], to_owner.at[h, b, own], o_send.at[h, b], o_recv.at[h, b],
                (line(h, q), col),
            )

    for n in range(2):
        inner[n] = jnp.zeros((EXPERTS * GROUP, EXPERTS * GROUP), F32)
    for h in range(2):
        for b in range(2):
            drain(terms.at[h, b], t_recv.at[h, b])
            drain(merged.at[h, b, 0:12], m_send.at[h, b])

    def gradients(h):
        @pl.loop(0, HALF // GROUP)
        def _(g):
            at = pl.multiple_of(g * GROUP, GROUP)
            chunk = experts[:, pl.ds(h * HALF + at, GROUP), :].reshape(EXPERTS * GROUP, LANES)
            out = None
            for b in range(2):
                term = terms[h, b, :, pl.ds(at, GROUP), :].reshape(EXPERTS * GROUP, LANES)
                part = dot_nn(spread_t[b], term)
                out = part if out is None else out + part
                inner[b] += dot_nt(term, chunk)
            merged[h, 0, :, pl.ds(at, GROUP), :] = out.astype(BF16).reshape(EXPERTS, GROUP, LANES)

        for n, dst in enumerate((gate_out, up_out, down_out)):
            pltpu.make_async_copy(
                merged.at[h, 0, :, :, pl.ds(n * BLOCK, BLOCK)],
                dst.at[:, pl.ds(h * HALF, HALF), :], out_sem.at[h, n],
            ).start()

    gradients(0)

    place = pl.ds(pl.multiple_of(k * (SEG // 2) + z * CHUNK, CHUNK), CHUNK)
    for b in range(2):
        for h in range(2):
            drain(to_owner.at[h, b, 0:3], o_recv.at[h, b])
        pieces = []
        for p in range(SIDE):
            for q in range(SIDE):
                one = to_owner[0, b, p, :, q * BLOCK:(q + 1) * BLOCK].astype(F32)
                two = to_owner[1, b, q, :, p * BLOCK:(p + 1) * BLOCK].astype(F32)
                pieces.append((one + two).astype(BF16))
        direct_all[b, place, :] = jnp.concatenate(pieces, axis=1)

        @pl.loop(1, DEPTH)
        def _(o):
            to = (z + o) % DEPTH
            send(
                direct_all.at[b, place], direct_all.at[b, place], a_send.at[b], a_recv.at[b],
                (row, to * 2 + k),
            )

    gradients(1)

    half = pl.ds(pl.multiple_of(k * (SEG // 2), SEG // 2), SEG // 2)
    for b in range(2):
        drain(direct_all.at[b, 0:7 * CHUNK], a_recv.at[b])
        send(direct_all.at[b, half], direct_all.at[b, half], f_send.at[b], f_recv.at[b], sibling)

    rows = lax.broadcasted_iota(jnp.int32, (EXPERTS * GROUP, EXPERTS * GROUP), 0)
    cols = lax.broadcasted_iota(jnp.int32, (EXPERTS * GROUP, EXPERTS * GROUP), 1)
    same = rows % GROUP == cols % GROUP
    for b in range(2):
        kept = jnp.where(same, inner[b], 0.0)
        inner_out[b] = jnp.sum(kept.reshape(EXPERTS, GROUP, EXPERTS * GROUP), axis=1)

    for b in range(2):
        drain(direct_all.at[b, 0:SEG // 2], f_recv.at[b])
    copy = pltpu.make_async_copy(direct_all, direct_out, e_sem.at[0])
    copy.start()

    for h in range(2):
        for o in range(SIDE - 1):
            drain(tokens.at[h, 0], tok_send.at[h, o])
            drain(tokens.at[h, 0], pass_send.at[h, o])
        for b in range(2):
            drain(deltas.at[h, 0:3], d_send.at[h, b])
            drain(depth_sum.at[h, 0:3], o_send.at[h, b])
        own = x if h == 0 else y

        @pl.loop(0, 8)
        def _(j):
            @pl.when(j % SIDE != own)
            def _():
                drain(part_out.at[h, 0], p_send.at[h, j])

            drain(weights.at[h, 0, 0:3], t_send.at[h, j])
            drain(to_depth.at[h, 0, 0:7], z_send.at[h, j])

        for n in range(3):
            drain(merged.at[h, 0, :, :, pl.ds(n * BLOCK, BLOCK)], out_sem.at[h, n])
    for n in range(4):
        drain(direct.at[0, 0], s_send.at[n])
    for b in range(2):
        drain(direct_all.at[b, 0:7 * CHUNK], a_send.at[b])
        drain(direct_all.at[b, 0:SEG // 2], f_send.at[b])
    copy.wait()


def moved(act, cot, gate_t, up_t, down, spread, spread_t):
    units = gate_t.shape[1]
    grad = jax.ShapeDtypeStruct((EXPERTS, units, BLOCK), BF16)
    vmem = pl.BlockSpec(memory_space=pltpu.VMEM)
    anywhere = pl.BlockSpec(memory_space=pl.ANY)
    dma = pltpu.SemaphoreType.DMA
    segs = SIDE * SIDE
    return pl.pallas_call(
        kernel,
        out_shape=(
            grad, grad, grad,
            jax.ShapeDtypeStruct((2, EXPERTS, EXPERTS * GROUP), F32),
            jax.ShapeDtypeStruct((2, SEG, 4 * WIDE), BF16),
        ),
        in_specs=[anywhere] * 5 + [vmem] * 2,
        out_specs=(anywhere, anywhere, anywhere, vmem, anywhere),
        scratch_shapes=[
            pltpu.VMEM((EXPERTS, 2 * HALF, LANES), BF16),
            pltpu.VMEM((2, 8, 2, SEG, WIDE), BF16),
            pltpu.VMEM((2, 2, segs, HALF, LANES), BF16),
            pltpu.VMEM((2, 8, SIDE, HALF, LANES), BF16),
            pltpu.VMEM((2, 2, segs, HALF, LANES), BF16),
            pltpu.VMEM((2, 8, 3, HALF, SEG), BF16),
            pltpu.VMEM((2, 2, 3, 3, HALF, SEG), BF16),
            pltpu.VMEM((2, 8, 3, HALF, SEG), BF16),
            pltpu.VMEM((4, 2, SEG // 2, WIDE), BF16),
            pltpu.VMEM((2, 8, SEG // 2, WIDE), BF16),
            pltpu.VMEM((2, 8, DEPTH, CHUNK, WIDE), BF16),
            pltpu.VMEM((2, 8, DEPTH - 1, CHUNK, WIDE), BF16),
            pltpu.VMEM((2, 8, CHUNK, WIDE), BF16),
            pltpu.VMEM((2, 2, SIDE, CHUNK, WIDE), BF16),
            pltpu.VMEM((2, SEG, 4 * WIDE), BF16),
            pltpu.VMEM((2, EXPERTS * GROUP, EXPERTS * GROUP), F32),
            dma((3,)), dma((2, 8)), dma((2, 3)), dma((2, 3)),
            dma((2, 2)), dma((2, 8)), dma((2, 8)), dma((2, 2)), dma((2, 2)), dma((2, 8)),
            dma((2, 8)), dma((2, 2)), dma((4,)), dma((2, 8)), dma((2, 8)), dma((2, 8)),
            dma((2, 2)), dma((2, 2)), dma((2,)), dma((2,)), dma((2,)), dma((2,)), dma((2, 3)),
        ],
        compiler_params=pltpu.CompilerParams(
            collective_id=1, has_side_effects=True, vmem_limit_bytes=63 * 2**20
        ),
        cost_estimate=pl.CostEstimate(flops=12 * 10**9, bytes_accessed=16 * 10**6, transcendentals=0),
        name="experts",
    )(act, cot, gate_t, up_t, down, spread, spread_t)


def shards(activations, cotangent, router, gate_experts, up_experts, down_experts, route_source):
    model_width = activations.shape[1]
    segs_here = activations.shape[0] // SEG
    seg_count = segs_here * lax.axis_size("row")
    first_seg = lax.axis_index("row") * segs_here
    own_means = jnp.mean(activations.reshape(segs_here, SEG, model_width), axis=1, dtype=F32)
    all_means = lax.all_gather(own_means, "row", axis=0, tiled=True)
    all_scores = jnp.dot(all_means, router, precision=PRECISE)
    chooser = (route_source[:, None] == jnp.arange(seg_count, dtype=jnp.int32)[None, :]).astype(F32)
    logits = jnp.dot(chooser, all_scores, precision=PRECISE)
    powers = jnp.exp(logits)
    routes = powers / jnp.sum(powers, axis=-1, keepdims=True)
    rounded = routes.astype(BF16)
    ordered = rounded.reshape(seg_count // 2, 2, EXPERTS).transpose(1, 0, 2)
    same = jnp.eye(GROUP, dtype=BF16)
    wide = EXPERTS * GROUP
    spread = (ordered[:, :, None, :, None] * same[None, None, :, None, :]).reshape(2, wide, wide)
    spread_t = spread.transpose(0, 2, 1)
    gate_t, up_t, down_t, inner, direct = moved(
        activations, cotangent, gate_experts.transpose(0, 2, 1), up_experts.transpose(0, 2, 1),
        down_experts, spread, spread_t,
    )
    partial_value = jnp.sum(inner.reshape(2, seg_count // 2, EXPERTS, GROUP), axis=-1)
    partial_value = partial_value.transpose(1, 0, 2).reshape(seg_count, EXPERTS)
    route_grad = lax.psum(partial_value, ("row", "col"))
    logit_grad = routes * (route_grad - jnp.sum(routes * route_grad, axis=-1, keepdims=True))
    source_grad = jnp.dot(chooser.T, logit_grad, precision=PRECISE)
    own_source = lax.dynamic_slice_in_dim(source_grad, first_seg, segs_here, 0)
    router_grad = jnp.dot(all_means.T, source_grad, precision=PRECISE)
    mean_grad = jnp.dot(own_source, router.T, precision=PRECISE)
    input_grad = (
        (direct.astype(F32) + mean_grad[:, None, :] / SEG).reshape(-1, model_width).astype(BF16)
    )
    return (
        input_grad, gate_t.transpose(0, 2, 1), up_t.transpose(0, 2, 1), down_t, router_grad,
    )


def solution(mesh):
    in_specs = (
        P("row", None),
        P("row", None),
        P(),
        P(None, "row", "col"),
        P(None, "row", "col"),
        P(None, "col", "row"),
        P(),
    )
    out_specs = (
        P("row", None),
        P(None, "row", "col"),
        P(None, "row", "col"),
        P(None, "col", "row"),
        P(),
    )
    return jax.shard_map(shards, mesh=mesh, in_specs=in_specs, out_specs=out_specs, check_vma=False)
```

```python
import functools

import jax
import jax.numpy as jnp
from jax import lax
from jax.experimental import pallas as pl
from jax.experimental.pallas import tpu as pltpu
from jax.sharding import PartitionSpec as P

SEG = 256
EXPERTS = 16
SIDE = 4
DEPTH = 8
BLOCK = 128
HALF = 176
LANES = 3 * BLOCK
WIDE = SIDE * BLOCK
GROUP = 16
CHUNK = 16
PIECE = 32
PRECISE = lax.Precision.HIGHEST
MESH = pl.DeviceIdType.MESH
F32 = jnp.float32
BF16 = jnp.bfloat16


def dot_nn(a, b):
    return lax.dot_general(a, b, (((1,), (0,)), ((), ())), preferred_element_type=F32)


def dot_nt(a, b):
    return lax.dot_general(a, b, (((1,), (1,)), ((), ())), preferred_element_type=F32)


def dot_tn(a, b):
    return lax.dot_general(a, b, (((0,), (0,)), ((), ())), preferred_element_type=F32)


def drain(ref, sem):
    pltpu.make_async_copy(ref, ref, sem).wait()


def kernel(
    act, cot, gate_t, up_t, down, router_t, wanted,
    gate_out, up_out, down_out, source_out, means_out, direct_out,
    experts, tokens, merged, weights, terms, part_out, part_in, deltas,
    direct, from_pair, to_depth, from_depth, depth_sum, to_owner, direct_all, inner,
    spread, spread_t, scores, means, routes, in_row, in_col, source, chooser,
    e_sem, tok_sem, tok_send, near_sem, near_send, pass_sem, pass_send, m_send, m_recv, p_send, p_recv, d_send, d_recv,
    t_send, t_recv, s_send, s_recv, z_send, z_recv, o_send, o_recv, a_send, a_recv,
    f_send, f_recv, out_sem, c_send, c_recv, n_send, n_recv, r_send, r_recv, l_send, l_recv,
):
    row = lax.axis_index("row")
    col = lax.axis_index("col")
    x, y = row // SIDE, row % SIDE
    z, k = col // 2, col % 2
    sibling = (row, z * 2 + 1 - k)

    def line(h, at):
        return jnp.where(h == 0, at * SIDE + y, x * SIDE + at)

    def cross(h, at):
        return jnp.where(h == 0, x * SIDE + at, at * SIDE + y)

    def send(src, dst, send_sem, recv_sem, to):
        pltpu.make_async_remote_copy(
            src_ref=src, dst_ref=dst, send_sem=send_sem, recv_sem=recv_sem,
            device_id=to, device_id_type=MESH,
        ).start()

    loads = [
        pltpu.make_async_copy(src, experts.at[:, :, pl.ds(n * BLOCK, BLOCK)], e_sem.at[n])
        for n, src in enumerate((gate_t, up_t, down))
    ]
    read = pltpu.make_async_copy(act, direct_all, out_sem.at[0, 0])
    read.start()
    for load in loads:
        load.start()

    rows_all = SIDE * SIDE
    cols_all = 2 * DEPTH
    barrier = pltpu.get_barrier_semaphore()

    @pl.loop(1, rows_all)
    def _(o):
        pl.semaphore_signal(
            barrier, inc=1, device_id=((row + o) % rows_all, col), device_id_type=MESH
        )

    @pl.loop(1, cols_all)
    def _(o):
        pl.semaphore_signal(
            barrier, inc=1, device_id=(row, (col + o) % cols_all), device_id_type=MESH
        )

    read.wait()
    found = []
    for b in range(2):
        def add(i, total):
            at = pl.multiple_of(b * SEG + i * GROUP, GROUP)
            return total + direct_all[pl.ds(at, GROUP), :].astype(F32)

        total = lax.fori_loop(0, SEG // GROUP, add, jnp.zeros((GROUP, 4 * WIDE), F32))
        found.append(jnp.sum(total, axis=0, keepdims=True) / SEG)
        for q in range(rows_all):
            means[row, b * rows_all + q:b * rows_all + q + 1, :] = found[b][:, q * BLOCK:(q + 1) * BLOCK]
    found.append(jnp.zeros((6, 4 * WIDE), F32))
    scores[row] = jnp.zeros((8, BLOCK), F32)
    scores[row, :, 0:EXPERTS] = lax.dot_general(
        jnp.concatenate(found, axis=0), router_t[...], (((1,), (1,)), ((), ())),
        precision=PRECISE, preferred_element_type=F32,
    )
    pl.semaphore_wait(barrier, rows_all + cols_all - 2)

    @pl.loop(1, rows_all)
    def _(o):
        send(scores.at[row], scores.at[row], c_send, c_recv, ((row + o) % rows_all, col))

    first = pl.multiple_of((k * SIDE + z % SIDE) * PIECE, PIECE)
    piece = pl.ds(first, PIECE)

    @pl.loop(0, 2)
    def _(b):
        rows = pl.ds(pl.multiple_of(b * SEG + first, PIECE), PIECE)
        for o in range(1, SIDE):
            for n, src in enumerate((act, cot)):
                to = (x + o) % SIDE
                j = SIDE * b + x
                send(
                    src.at[rows, pl.ds(pl.multiple_of(to * WIDE, WIDE), WIDE)],
                    tokens.at[0, j, n, piece], tok_send, tok_sem.at[0, j], (to * SIDE + y, col),
                )
                to = (y + o) % SIDE
                j = SIDE * b + y
                for q in range(SIDE):
                    send(
                        src.at[rows, pl.ds(pl.multiple_of((q * SIDE + to) * BLOCK, BLOCK), BLOCK)],
                        tokens.at[1, j, n, piece, pl.ds(q * BLOCK, BLOCK)],
                        tok_send, tok_sem.at[1, j], (x * SIDE + to, col),
                    )

    for b in range(2):
        rows = pl.ds(b * SEG, SEG)
        for n, src in enumerate((act, cot)):
            pltpu.make_async_copy(
                src.at[rows, pl.ds(pl.multiple_of(x * WIDE, WIDE), WIDE)],
                tokens.at[0, SIDE * b + x, n], tok_sem.at[0, SIDE * b + x],
            ).start()
            for q in range(SIDE):
                pltpu.make_async_copy(
                    src.at[rows, pl.ds(pl.multiple_of((q * SIDE + y) * BLOCK, BLOCK), BLOCK)],
                    tokens.at[1, SIDE * b + y, n, :, pl.ds(q * BLOCK, BLOCK)],
                    tok_sem.at[1, SIDE * b + y],
                ).start()
    for s in range(2 * rows_all):
        at = (s % 2) * rows_all + s // 2
        v = wanted[s]
        place = (v // 2) * 8 + v % 2
        lanes = lax.broadcasted_iota(jnp.int32, (1, BLOCK), 1)
        chooser[at:at + 1, :] = jnp.where(lanes == place, 1.0, 0.0).astype(F32)

    drain(scores.at[0:rows_all - 1], c_recv)
    logits = lax.dot_general(
        chooser[...], scores[...].reshape(rows_all * 8, BLOCK), (((1,), (0,)), ((), ())),
        precision=PRECISE, preferred_element_type=F32,
    )
    real = lax.broadcasted_iota(jnp.int32, logits.shape, 1) < EXPERTS
    powers = jnp.where(real, jnp.exp(logits), 0.0)
    routes[...] = powers / jnp.sum(powers, axis=1, keepdims=True)
    span = EXPERTS * GROUP

    def iota(shape, axis):
        return lax.broadcasted_iota(jnp.int32, shape, axis)

    same = iota((span, span), 0) % GROUP == iota((span, span), 1) % GROUP
    pick = (iota((span, rows_all), 0) // GROUP == iota((span, rows_all), 1)).astype(BF16)
    expand = (iota((span, BLOCK), 0) // GROUP == iota((span, BLOCK), 1)).astype(BF16)
    for b in range(2):
        rounded = routes[b * rows_all:(b + 1) * rows_all, :].astype(BF16)
        long = dot_nt(dot_nn(pick, rounded).astype(BF16), expand)
        spread[b] = jnp.where(same, long, 0.0).astype(BF16)
        long = dot_nt(dot_nt(expand, rounded).astype(BF16), pick)
        spread_t[b] = jnp.where(same, long, 0.0).astype(BF16)

    def others(b, h):
        own = x if h == 0 else y
        return [SIDE * b + (own + o) % SIDE for o in range(1, SIDE)]

    for b in range(2):
        for o in range(SIDE - 1):
            for h in range(2):
                j = others(b, h)[o]
                drain(tokens.at[0, 0, :, 0:PIECE], tok_sem.at[h, j])
                both = tokens.at[h, j, :, piece]
                for step in (1, DEPTH - 1):
                    to = (row, (z + step) % DEPTH * 2 + k)
                    send(both, both, near_send.at[0], near_sem.at[h, j], to)
                for n, step in enumerate((2, DEPTH - 2)):
                    one = tokens.at[h, j, n, piece]
                    to = (row, (z + step) % DEPTH * 2 + k)
                    send(one, one, near_send.at[1], near_sem.at[h, j], to)
    for load in loads:
        load.wait()

    for b in range(2):
        for h in range(2):

            @pl.loop(0, HALF // GROUP)
            def _(g):
                at = pl.multiple_of(g * GROUP, GROUP)
                chunk = experts[:, pl.ds(h * HALF + at, GROUP), :].reshape(EXPERTS * GROUP, LANES)
                out = dot_nn(spread[b], chunk).astype(BF16)
                merged[h, b, :, pl.ds(at, GROUP), :] = out.reshape(SIDE * SIDE, GROUP, LANES)

            own = x if h == 0 else y
            side = y if h == 0 else x

            @pl.loop(0, SIDE)
            def _(t):
                q = (own + 1 + t) % SIDE
                for o in range(SIDE):
                    to = (side + o) % SIDE
                    slot = q * SIDE + to if h == 0 else to * SIDE + q
                    src = merged.at[h, b, slot]
                    dst = weights.at[h, SIDE * b + q, side]
                    if o == 0:
                        pltpu.make_async_copy(src, dst, m_recv.at[h, SIDE * b + q]).start()
                    else:
                        device = x * SIDE + to if h == 0 else to * SIDE + y
                        send(src, dst, m_send.at[h, b], m_recv.at[h, SIDE * b + q], (device, col))

    def joined(h, j, n):
        return jnp.concatenate(
            [weights[h, j, q, :, n * BLOCK:(n + 1) * BLOCK] for q in range(SIDE)], axis=1
        )

    def forward(b):
        own_half = pl.ds(pl.multiple_of(k * (SEG // 2), SEG // 2), SEG // 2)
        for o in range(SIDE - 1):
            for h in range(2):
                j = others(b, h)[o]
                drain(tokens.at[0, 0, :, 0:3 * PIECE], near_sem.at[h, j])
                part = tokens.at[h, j, :, own_half]
                send(part, part, pass_send.at[b], pass_sem.at[h, j], sibling)

        @pl.loop(0, 8)
        def _(i):
            t, h = i // 2, i % 2
            own = jnp.where(h == 0, x, y)
            q = (own + 1 + t) % SIDE
            j = SIDE * b + q
            drain(weights.at[h, j], m_recv.at[h, j])

            @pl.when(t < SIDE - 1)
            def _():
                drain(tokens.at[0, 0, :, 0:SEG // 2], pass_sem.at[h, j])

            @pl.when(t == SIDE - 1)
            def _():
                drain(tokens.at[h, j], tok_sem.at[h, j])

            for n in range(3):
                side = tokens[h, j, 0 if n < 2 else 1]
                part_out[h, j, n] = dot_nt(joined(h, j, n), side).astype(BF16)

            @pl.when(t < SIDE - 1)
            def _():
                send(
                    part_out.at[h, j], part_in.at[h, b, t], p_send.at[h, j], p_recv.at[h, b],
                    (line(h, q), col),
                )

    forward(0)
    forward(1)

    @pl.loop(0, 4)
    def _(i):
        b, h = i // 2, i % 2
        own = jnp.where(h == 0, x, y)
        j = SIDE * b + own
        drain(part_in.at[h, b], p_recv.at[h, b])

        def total(n):
            out = part_out[h, j, n].astype(F32)
            for o in range(SIDE - 1):
                out += part_in[h, b, o, n].astype(F32)
            return out

        gate, up, grad = total(0), total(1), total(2)
        sig = jax.nn.sigmoid(gate)
        gated = gate * sig
        deltas[h, j, 0] = (grad * up * sig * (1.0 + gate * (1.0 - sig))).astype(BF16)
        deltas[h, j, 1] = (grad * gated).astype(BF16)
        deltas[h, j, 2] = (gated * up).astype(BF16)
        for o in range(1, SIDE):
            send(
                deltas.at[h, j], deltas.at[h, j], d_send.at[h, b], d_recv.at[h, j],
                (line(h, (own + o) % SIDE), col),
            )

    def item(i):
        b, t, h = i // 8, (i // 2) % SIDE, i % 2
        own = jnp.where(h == 0, x, y)
        q = (own + t) % SIDE
        return b, t, h, q, SIDE * b + q

    def pair_sum(i):
        b, t, h, q, j = item(i)
        drain(from_pair.at[h, j], s_recv.at[h, j])
        out = direct[i % 4, k].astype(F32) + from_pair[h, j].astype(F32)
        to_depth[h, j] = out.astype(BF16).reshape(DEPTH, CHUNK, WIDE)

        @pl.loop(1, DEPTH)
        def _(o):
            to = (z + o) % DEPTH
            send(
                to_depth.at[h, j, to], from_depth.at[h, j, o - 1], z_send.at[h, j], z_recv.at[h, j],
                (row, to * 2 + k),
            )

    def send_terms(i):
        b, t, h, q, j = item(i)
        side = jnp.where(h == 0, y, x)
        slot = jnp.where(h == 0, q * SIDE + y, x * SIDE + q)
        for o in range(1, SIDE):
            to = (side + o) % SIDE
            send(
                weights.at[h, j, to], terms.at[h, b, slot], t_send.at[h, j], t_recv.at[h, b],
                (cross(h, to), col),
            )
        pltpu.make_async_copy(weights.at[h, j, side], terms.at[h, b, slot], t_recv.at[h, b]).start()

    def backward(i):
        b, t, h, q, j = item(i)

        @pl.when(t > 0)
        def _():
            drain(deltas.at[h, j], d_recv.at[h, j])

        @pl.when(i >= 4)
        def _():
            drain(direct.at[0, 0], s_send.at[i % 4])

        both = deltas[h, j, 0:2].reshape(2 * HALF, SEG)
        out = dot_tn(both, jnp.concatenate([joined(h, j, 0), joined(h, j, 1)], axis=0))
        direct[i % 4] = out.astype(BF16).reshape(2, SEG // 2, WIDE)
        send(direct.at[i % 4, 1 - k], from_pair.at[h, j], s_send.at[i % 4], s_recv.at[h, j], sibling)

        for n in range(3):
            side = tokens[h, j, 0 if n < 2 else 1]
            out = dot_nn(deltas[h, j, n], side).astype(BF16)
            for p in range(SIDE):
                weights[h, j, p, :, n * BLOCK:(n + 1) * BLOCK] = out[:, p * BLOCK:(p + 1) * BLOCK]

        @pl.when(i > 0)
        def _():
            pair_sum(i - 1)

    @pl.loop(0, 8)
    def _(i):
        backward(i)
        send_terms(i)

    @pl.loop(8, 16)
    def _(i):
        backward(i)

    pair_sum(15)

    def depth_sums(b):
        @pl.loop(0, 8)
        def _(i):
            _, t, h, q, j = item(b * 8 + i)
            drain(from_depth.at[h, j], z_recv.at[h, j])
            out = to_depth[h, j, z].astype(F32)
            for o in range(DEPTH - 1):
                out += from_depth[h, j, o].astype(F32)
            depth_sum[h, j] = out.astype(BF16)
            own = jnp.where(h == 0, x, y)

            @pl.when(t == 0)
            def _():
                to_owner[h, b, own] = out.astype(BF16)

            @pl.when(t > 0)
            def _():
                send(
                    depth_sum.at[h, j], to_owner.at[h, b, own], o_send.at[h, b], o_recv.at[h, b],
                    (line(h, q), col),
                )

    def place(b):
        return pl.ds(pl.multiple_of(b * SEG + k * (SEG // 2) + z * CHUNK, CHUNK), CHUNK)

    def half(b):
        return pl.ds(pl.multiple_of(b * SEG + k * (SEG // 2), SEG // 2), SEG // 2)

    def spread_direct(b):
        for h in range(2):
            drain(to_owner.at[h, b, 0:3], o_recv.at[h, b])
        pieces = []
        for p in range(SIDE):
            for q in range(SIDE):
                one = to_owner[0, b, p, :, q * BLOCK:(q + 1) * BLOCK].astype(F32)
                two = to_owner[1, b, q, :, p * BLOCK:(p + 1) * BLOCK].astype(F32)
                pieces.append((one + two).astype(BF16))
        direct_all[place(b), :] = jnp.concatenate(pieces, axis=1)

        @pl.loop(1, DEPTH)
        def _(o):
            to = (z + o) % DEPTH
            send(
                direct_all.at[place(b)], direct_all.at[place(b)], a_send.at[b], a_recv.at[b],
                (row, to * 2 + k),
            )

    def share_direct(b):
        drain(direct_all.at[0:7 * CHUNK], a_recv.at[b])
        send(direct_all.at[half(b)], direct_all.at[half(b)], f_send.at[b], f_recv.at[b], sibling)

    def group(h, g):
        at = pl.multiple_of(g * GROUP, GROUP)
        return at, experts[:, pl.ds(h * HALF + at, GROUP), :].reshape(span, LANES)

    def products(b):
        inner[b] = jnp.zeros((span, span), F32)
        for h in range(2):
            drain(terms.at[h, b], t_recv.at[h, b])

            @pl.loop(0, HALF // GROUP)
            def _(g):
                at, chunk = group(h, g)
                term = terms[h, b, :, pl.ds(at, GROUP), :].reshape(span, LANES)
                inner[b] += dot_nt(term, chunk)

    def gradients(h):
        for b in range(2):
            drain(merged.at[h, b, 0:12], m_send.at[h, b])

        @pl.loop(0, HALF // GROUP)
        def _(g):
            at = pl.multiple_of(g * GROUP, GROUP)
            out = None
            for b in range(2):
                term = terms[h, b, :, pl.ds(at, GROUP), :].reshape(span, LANES)
                part = dot_nn(spread_t[b], term)
                out = part if out is None else out + part
            merged[h, 0, :, pl.ds(at, GROUP), :] = out.astype(BF16).reshape(EXPERTS, GROUP, LANES)

        for n, dst in enumerate((gate_out, up_out, down_out)):
            pltpu.make_async_copy(
                merged.at[h, 0, :, :, pl.ds(n * BLOCK, BLOCK)],
                dst.at[:, pl.ds(h * HALF, HALF), :], out_sem.at[h, n],
            ).start()

    depth_sums(0)
    pl.loop(8, 12)(send_terms)
    spread_direct(0)
    depth_sums(1)
    pl.loop(12, 16)(send_terms)
    spread_direct(1)
    share_direct(0)
    products(0)
    products(1)

    fold = (iota((span, BLOCK), 0) // GROUP == iota((span, BLOCK), 1) % EXPERTS).astype(F32)
    here = iota((rows_all, BLOCK), 1) // EXPERTS == iota((rows_all, BLOCK), 0) % 8
    packed = []
    for b in range(2):
        kept = jnp.sum(jnp.where(same, inner[b], 0.0).reshape(EXPERTS, GROUP, span), axis=1)
        dense = lax.dot_general(
            kept, fold, (((1,), (0,)), ((), ())), precision=PRECISE, preferred_element_type=F32
        )
        packed.append(jnp.sum(jnp.where(here, dense, 0.0).reshape(2, 8, BLOCK), axis=1))
    packed.append(jnp.zeros((4, BLOCK), F32))
    in_row[0] = jnp.concatenate(packed, axis=0)

    @pl.loop(1, rows_all)
    def _(o):
        send(in_row.at[0], in_row.at[o], r_send, r_recv, ((row + o) % rows_all, col))

    gradients(0)
    share_direct(1)
    drain(in_row.at[1:rows_all], r_recv)

    @pl.loop(1, rows_all)
    def _(o):
        send(means.at[row], means.at[row], n_send, n_recv, ((row + o) % rows_all, col))

    out = in_row[0]
    for o in range(1, rows_all):
        out += in_row[o]
    in_col[0] = out

    @pl.loop(1, cols_all)
    def _(o):
        send(in_col.at[0], in_col.at[o], l_send, l_recv, (row, (col + o) % cols_all))

    gradients(1)
    for b in range(2):
        drain(direct_all.at[0:SEG // 2], f_recv.at[b])
    copy = pltpu.make_async_copy(direct_all, direct_out, e_sem.at[0])
    copy.start()
    drain(in_col.at[1:cols_all], l_recv)
    out = in_col[0]
    for o in range(1, cols_all):
        out += in_col[o]
    wide = jnp.concatenate(
        [jnp.broadcast_to(out[p:p + 1, :], (8, BLOCK)) for p in range(4)], axis=0
    )
    shape = (2 * rows_all, BLOCK)
    wide = jnp.where(iota(shape, 1) // EXPERTS == iota(shape, 0) % 8, wide, 0.0)
    narrow = (iota((BLOCK, BLOCK), 0) % EXPERTS == iota((BLOCK, BLOCK), 1)).astype(F32)
    total = lax.dot_general(
        wide, narrow, (((1,), (0,)), ((), ())), precision=PRECISE, preferred_element_type=F32
    )
    logit_grad = routes[...] * (total - jnp.sum(routes[...] * total, axis=1, keepdims=True))
    source[...] = lax.dot_general(
        chooser[...], logit_grad, (((0,), (0,)), ((), ())),
        precision=PRECISE, preferred_element_type=F32,
    ).reshape(rows_all, 8, BLOCK)
    source_out[...] = source[...]
    drain(means.at[0:rows_all - 1], n_recv)
    means_out[...] = means[...]

    for h in range(2):
        for b in range(2):
            drain(deltas.at[h, 0:3], d_send.at[h, b])
            drain(depth_sum.at[h, 0:3], o_send.at[h, b])
        own = x if h == 0 else y

        @pl.loop(0, 8)
        def _(j):
            @pl.when(j % SIDE != own)
            def _():
                drain(part_out.at[h, 0], p_send.at[h, j])

            drain(weights.at[h, 0, 0:3], t_send.at[h, j])
            drain(to_depth.at[h, 0, 0:7], z_send.at[h, j])

        for n in range(3):
            drain(merged.at[h, 0, :, :, pl.ds(n * BLOCK, BLOCK)], out_sem.at[h, n])
    for n in range(4):
        drain(direct.at[0, 0], s_send.at[n])
    drain(tokens.at[0, 0:3, 0], tok_send)
    drain(tokens.at[0, 0:3], near_send.at[0])
    drain(tokens.at[0, 0:3, 0], near_send.at[1])
    for b in range(2):
        drain(tokens.at[0, 0:3], pass_send.at[b])
        drain(direct_all.at[0:7 * CHUNK], a_send.at[b])
        drain(direct_all.at[0:SEG // 2], f_send.at[b])
    drain(scores.at[0:rows_all - 1], c_send)
    drain(means.at[0:rows_all - 1], n_send)
    drain(in_row.at[1:rows_all], r_send)
    drain(in_col.at[1:cols_all], l_send)
    copy.wait()


def moved(act, cot, gate_t, up_t, down, router_t, wanted):
    units = gate_t.shape[1]
    grad = jax.ShapeDtypeStruct((EXPERTS, units, BLOCK), BF16)
    vmem = pl.BlockSpec(memory_space=pltpu.VMEM)
    anywhere = pl.BlockSpec(memory_space=pl.ANY)
    dma = pltpu.SemaphoreType.DMA
    segs = SIDE * SIDE
    return pl.pallas_call(
        kernel,
        out_shape=(
            grad, grad, grad,
            jax.ShapeDtypeStruct((segs, 8, BLOCK), F32),
            jax.ShapeDtypeStruct((segs, 2 * segs, BLOCK), F32),
            jax.ShapeDtypeStruct((2 * SEG, 4 * WIDE), BF16),
        ),
        in_specs=[anywhere] * 5 + [vmem, pl.BlockSpec(memory_space=pltpu.SMEM)],
        out_specs=(anywhere, anywhere, anywhere, vmem, vmem, anywhere),
        scratch_shapes=[
            pltpu.VMEM((EXPERTS, 2 * HALF, LANES), BF16),
            pltpu.VMEM((2, 8, 2, SEG, WIDE), BF16),
            pltpu.VMEM((2, 2, segs, HALF, LANES), BF16),
            pltpu.VMEM((2, 8, SIDE, HALF, LANES), BF16),
            pltpu.VMEM((2, 2, segs, HALF, LANES), BF16),
            pltpu.VMEM((2, 8, 3, HALF, SEG), BF16),
            pltpu.VMEM((2, 2, 3, 3, HALF, SEG), BF16),
            pltpu.VMEM((2, 8, 3, HALF, SEG), BF16),
            pltpu.VMEM((4, 2, SEG // 2, WIDE), BF16),
            pltpu.VMEM((2, 8, SEG // 2, WIDE), BF16),
            pltpu.VMEM((2, 8, DEPTH, CHUNK, WIDE), BF16),
            pltpu.VMEM((2, 8, DEPTH - 1, CHUNK, WIDE), BF16),
            pltpu.VMEM((2, 8, CHUNK, WIDE), BF16),
            pltpu.VMEM((2, 2, SIDE, CHUNK, WIDE), BF16),
            pltpu.VMEM((2 * SEG, 4 * WIDE), BF16),
            pltpu.VMEM((2, EXPERTS * GROUP, EXPERTS * GROUP), F32),
            pltpu.VMEM((2, EXPERTS * GROUP, EXPERTS * GROUP), BF16),
            pltpu.VMEM((2, EXPERTS * GROUP, EXPERTS * GROUP), BF16),
            pltpu.VMEM((segs, 8, BLOCK), F32),
            pltpu.VMEM((segs, 2 * segs, BLOCK), F32),
            pltpu.VMEM((2 * segs, BLOCK), F32),
            pltpu.VMEM((segs, 8, BLOCK), F32),
            pltpu.VMEM((2 * DEPTH, 8, BLOCK), F32),
            pltpu.VMEM((segs, 8, BLOCK), F32),
            pltpu.VMEM((2 * segs, BLOCK), F32),
            dma((3,)), dma((2, 8)), dma, dma((2, 8)), dma((2,)), dma((2, 8)), dma((2,)),
            dma((2, 2)), dma((2, 8)), dma((2, 8)), dma((2, 2)), dma((2, 2)), dma((2, 8)),
            dma((2, 8)), dma((2, 2)), dma((4,)), dma((2, 8)), dma((2, 8)), dma((2, 8)),
            dma((2, 2)), dma((2, 2)), dma((2,)), dma((2,)), dma((2,)), dma((2,)), dma((2, 3)),
            dma, dma, dma, dma, dma, dma, dma, dma,
        ],
        compiler_params=pltpu.CompilerParams(
            collective_id=1, has_side_effects=True, vmem_limit_bytes=63 * 2**20
        ),
        cost_estimate=pl.CostEstimate(flops=12 * 10**9, bytes_accessed=16 * 10**6, transcendentals=0),
        name="experts",
    )(act, cot, gate_t, up_t, down, router_t, wanted)


def finish_kernel(
    gate, up, down, direct, source, means, router_t,
    gate_out, up_out, down_out, input_out, router_out, grads, rows, in_sem, out_sem,
):
    parts = in_sem.shape[1]
    pairs = ((gate, gate_out), (up, up_out), (down, down_out))

    def pieces(n, p, size):
        at = pl.ds(p * (size // parts), size // parts)
        if n == 3:
            return direct.at[at], rows.at[at], input_out.at[at]
        return pairs[n][0].at[at], grads.at[n, at], pairs[n][1].at[at]

    sizes = [EXPERTS] * 3 + [rows.shape[0]]
    order = [(n, p) for p in range(parts) for n in (3, 0, 1, 2)]
    for n, p in order:
        src, mid, _ = pieces(n, p, sizes[n])
        pltpu.make_async_copy(src, mid, in_sem.at[n, p]).start()
    own = source[lax.axis_index("row")]
    mean_grad = lax.dot_general(
        own[:, 0:EXPERTS], router_t[...], (((1,), (0,)), ((), ())),
        precision=PRECISE, preferred_element_type=F32,
    ) / SEG
    for n, p in order:
        src, mid, dst = pieces(n, p, sizes[n])
        pltpu.make_async_copy(src, mid, in_sem.at[n, p]).wait()
        if n == 3:
            size = sizes[n] // parts
            extra = mean_grad[p * size // SEG:p * size // SEG + 1, :]

            @pl.loop(0, size // GROUP)
            def _(i):
                at = pl.ds(pl.multiple_of(p * size + i * GROUP, GROUP), GROUP)
                rows[at, :] = (rows[at, :].astype(F32) + extra).astype(BF16)

        pltpu.make_async_copy(mid, dst, out_sem.at[n, p]).start()
    segs = means.shape[0]
    for q in range(segs):
        out = None
        for b in range(2):
            part = lax.dot_general(
                source[:, b, :], means[:, b * segs + q, :], (((0,), (0,)), ((), ())),
                precision=PRECISE, preferred_element_type=F32,
            )
            out = part if out is None else out + part
        router_out[:, q * BLOCK:(q + 1) * BLOCK] = out[0:EXPERTS, :]
    for n, p in order:
        _, mid, dst = pieces(n, p, sizes[n])
        pltpu.make_async_copy(mid, dst, out_sem.at[n, p]).wait()


def finish(gate, up, down, direct, source, means, router_t):
    vmem = pl.BlockSpec(memory_space=pltpu.VMEM)
    anywhere = pl.BlockSpec(memory_space=pl.ANY)
    like = [jax.ShapeDtypeStruct(v.shape, v.dtype) for v in (gate, up, down, direct)]
    return pl.pallas_call(
        finish_kernel,
        out_shape=(*like, jax.ShapeDtypeStruct(router_t.shape, F32)),
        in_specs=[anywhere] * 4 + [vmem] * 3,
        out_specs=(anywhere,) * 4 + (vmem,),
        scratch_shapes=[
            pltpu.VMEM((3, *gate.shape), BF16),
            pltpu.VMEM(direct.shape, BF16),
            pltpu.SemaphoreType.DMA((4, 4)),
            pltpu.SemaphoreType.DMA((4, 4)),
        ],
        compiler_params=pltpu.CompilerParams(vmem_limit_bytes=60 * 2**20),
        name="finish",
    )(gate, up, down, direct, source, means, router_t)


def shards(activations, cotangent, router, gate_experts, up_experts, down_experts, route_source):
    router_t = router.T
    gate_t, up_t, down_t, source, means, direct = moved(
        activations, cotangent, gate_experts.transpose(0, 2, 1), up_experts.transpose(0, 2, 1),
        down_experts, router_t, route_source,
    )
    gate_t, up_t, down_t, input_grad, router_grad = finish(
        gate_t, up_t, down_t, direct, source, means, router_t
    )
    return (
        input_grad, gate_t.transpose(0, 2, 1), up_t.transpose(0, 2, 1), down_t, router_grad.T,
    )


def solution(mesh):
    in_specs = (
        P("row", None),
        P("row", None),
        P(),
        P(None, "row", "col"),
        P(None, "row", "col"),
        P(None, "col", "row"),
        P(),
    )
    out_specs = (
        P("row", None),
        P(None, "row", "col"),
        P(None, "row", "col"),
        P(None, "col", "row"),
        P(),
    )
    return jax.shard_map(shards, mesh=mesh, in_specs=in_specs, out_specs=out_specs, check_vma=False)
```

```python
import functools

import jax
import jax.numpy as jnp
from jax import lax
from jax.experimental import pallas as pl
from jax.experimental.pallas import tpu as pltpu
from jax.sharding import PartitionSpec as P

SEG = 256
EXPERTS = 16
SIDE = 4
DEPTH = 8
BLOCK = 128
HALF = 176
LANES = 3 * BLOCK
WIDE = SIDE * BLOCK
GROUP = 16
CHUNK = 16
PIECE = 32
PRECISE = lax.Precision.HIGHEST
MESH = pl.DeviceIdType.MESH
F32 = jnp.float32
BF16 = jnp.bfloat16


def dot_nn(a, b):
    return lax.dot_general(a, b, (((1,), (0,)), ((), ())), preferred_element_type=F32)


def dot_nt(a, b):
    return lax.dot_general(a, b, (((1,), (1,)), ((), ())), preferred_element_type=F32)


def dot_tn(a, b):
    return lax.dot_general(a, b, (((0,), (0,)), ((), ())), preferred_element_type=F32)


def drain(ref, sem):
    pltpu.make_async_copy(ref, ref, sem).wait()


def kernel(
    act, cot, gate_t, up_t, down, router_t, wanted,
    gate_out, up_out, down_out, source_out, means_out, direct_out,
    experts, tokens, merged, weights, terms, part_out, part_in, deltas,
    direct, from_pair, to_depth, from_depth, depth_sum, to_owner, direct_all, inner,
    spread, spread_t, scores, means, routes, in_row, in_col, source, chooser,
    e_sem, tok_sem, tok_send, near_sem, near_send, pass_sem, pass_send, m_send, m_recv, p_send, p_recv, d_send, d_recv, d_pass,
    t_send, t_recv, s_send, s_recv, z_send, z_recv, z_pass, o_send, o_recv, a_send, a_recv, a_pass,
    f_send, f_recv, out_sem, c_send, c_recv, n_send, n_recv, r_send, r_recv, l_send, l_recv,
):
    row = lax.axis_index("row")
    col = lax.axis_index("col")
    x, y = row // SIDE, row % SIDE
    z, k = col // 2, col % 2
    sibling = (row, z * 2 + 1 - k)

    def line(h, at):
        return jnp.where(h == 0, at * SIDE + y, x * SIDE + at)

    def cross(h, at):
        return jnp.where(h == 0, x * SIDE + at, at * SIDE + y)

    def send(src, dst, send_sem, recv_sem, to):
        pltpu.make_async_remote_copy(
            src_ref=src, dst_ref=dst, send_sem=send_sem, recv_sem=recv_sem,
            device_id=to, device_id_type=MESH,
        ).start()

    loads = [
        pltpu.make_async_copy(src, experts.at[:, :, pl.ds(n * BLOCK, BLOCK)], e_sem.at[n])
        for n, src in enumerate((gate_t, up_t, down))
    ]
    read = pltpu.make_async_copy(act, direct_all, out_sem.at[0, 0])
    read.start()
    for load in loads:
        load.start()

    rows_all = SIDE * SIDE
    cols_all = 2 * DEPTH
    barrier = pltpu.get_barrier_semaphore()

    @pl.loop(1, rows_all)
    def _(o):
        pl.semaphore_signal(
            barrier, inc=1, device_id=((row + o) % rows_all, col), device_id_type=MESH
        )

    @pl.loop(1, cols_all)
    def _(o):
        pl.semaphore_signal(
            barrier, inc=1, device_id=(row, (col + o) % cols_all), device_id_type=MESH
        )

    read.wait()
    found = []
    for b in range(2):
        def add(i, total):
            at = pl.multiple_of(b * SEG + i * GROUP, GROUP)
            return total + direct_all[pl.ds(at, GROUP), :].astype(F32)

        total = lax.fori_loop(0, SEG // GROUP, add, jnp.zeros((GROUP, 4 * WIDE), F32))
        found.append(jnp.sum(total, axis=0, keepdims=True) / SEG)
        for q in range(rows_all):
            means[row, b * rows_all + q:b * rows_all + q + 1, :] = found[b][:, q * BLOCK:(q + 1) * BLOCK]
    found.append(jnp.zeros((6, 4 * WIDE), F32))
    scores[row] = jnp.zeros((8, BLOCK), F32)
    scores[row, :, 0:EXPERTS] = lax.dot_general(
        jnp.concatenate(found, axis=0), router_t[...], (((1,), (1,)), ((), ())),
        precision=PRECISE, preferred_element_type=F32,
    )
    pl.semaphore_wait(barrier, rows_all + cols_all - 2)

    @pl.loop(1, rows_all)
    def _(o):
        send(scores.at[row], scores.at[row], c_send, c_recv, ((row + o) % rows_all, col))

    first = pl.multiple_of((k * SIDE + z % SIDE) * PIECE, PIECE)
    piece = pl.ds(first, PIECE)

    @pl.loop(0, 2)
    def _(b):
        rows = pl.ds(pl.multiple_of(b * SEG + first, PIECE), PIECE)
        for o in range(1, SIDE):
            for n, src in enumerate((act, cot)):
                to = (x + o) % SIDE
                j = SIDE * b + x
                send(
                    src.at[rows, pl.ds(pl.multiple_of(to * WIDE, WIDE), WIDE)],
                    tokens.at[0, j, n, piece], tok_send, tok_sem.at[0, j], (to * SIDE + y, col),
                )
                to = (y + o) % SIDE
                j = SIDE * b + y
                for q in range(SIDE):
                    send(
                        src.at[rows, pl.ds(pl.multiple_of((q * SIDE + to) * BLOCK, BLOCK), BLOCK)],
                        tokens.at[1, j, n, piece, pl.ds(q * BLOCK, BLOCK)],
                        tok_send, tok_sem.at[1, j], (x * SIDE + to, col),
                    )

    for b in range(2):
        rows = pl.ds(b * SEG, SEG)
        for n, src in enumerate((act, cot)):
            pltpu.make_async_copy(
                src.at[rows, pl.ds(pl.multiple_of(x * WIDE, WIDE), WIDE)],
                tokens.at[0, SIDE * b + x, n], tok_sem.at[0, SIDE * b + x],
            ).start()
            for q in range(SIDE):
                pltpu.make_async_copy(
                    src.at[rows, pl.ds(pl.multiple_of((q * SIDE + y) * BLOCK, BLOCK), BLOCK)],
                    tokens.at[1, SIDE * b + y, n, :, pl.ds(q * BLOCK, BLOCK)],
                    tok_sem.at[1, SIDE * b + y],
                ).start()
    for s in range(2 * rows_all):
        at = (s % 2) * rows_all + s // 2
        v = wanted[s]
        place = (v // 2) * 8 + v % 2
        lanes = lax.broadcasted_iota(jnp.int32, (1, BLOCK), 1)
        chooser[at:at + 1, :] = jnp.where(lanes == place, 1.0, 0.0).astype(F32)

    drain(scores.at[0:rows_all - 1], c_recv)
    logits = lax.dot_general(
        chooser[...], scores[...].reshape(rows_all * 8, BLOCK), (((1,), (0,)), ((), ())),
        precision=PRECISE, preferred_element_type=F32,
    )
    real = lax.broadcasted_iota(jnp.int32, logits.shape, 1) < EXPERTS
    powers = jnp.where(real, jnp.exp(logits), 0.0)
    routes[...] = powers / jnp.sum(powers, axis=1, keepdims=True)
    span = EXPERTS * GROUP

    def iota(shape, axis):
        return lax.broadcasted_iota(jnp.int32, shape, axis)

    same = iota((span, span), 0) % GROUP == iota((span, span), 1) % GROUP
    pick = (iota((span, rows_all), 0) // GROUP == iota((span, rows_all), 1)).astype(BF16)
    expand = (iota((span, BLOCK), 0) // GROUP == iota((span, BLOCK), 1)).astype(BF16)
    for b in range(2):
        rounded = routes[b * rows_all:(b + 1) * rows_all, :].astype(BF16)
        long = dot_nt(dot_nn(pick, rounded).astype(BF16), expand)
        spread[b] = jnp.where(same, long, 0.0).astype(BF16)
        long = dot_nt(dot_nt(expand, rounded).astype(BF16), pick)
        spread_t[b] = jnp.where(same, long, 0.0).astype(BF16)

    def others(b, h):
        own = x if h == 0 else y
        return [SIDE * b + (own + o) % SIDE for o in range(1, SIDE)]

    for b in range(2):
        for o in range(SIDE - 1):
            for h in range(2):
                j = others(b, h)[o]
                drain(tokens.at[0, 0, :, 0:PIECE], tok_sem.at[h, j])
                both = tokens.at[h, j, :, piece]
                for step in (1, DEPTH - 1):
                    to = (row, (z + step) % DEPTH * 2 + k)
                    send(both, both, near_send.at[0], near_sem.at[h, j], to)
                for n, step in enumerate((2, DEPTH - 2)):
                    one = tokens.at[h, j, n, piece]
                    to = (row, (z + step) % DEPTH * 2 + k)
                    send(one, one, near_send.at[1], near_sem.at[h, j], to)
    for load in loads:
        load.wait()

    for b in range(2):
        for h in range(2):

            @pl.loop(0, HALF // GROUP)
            def _(g):
                at = pl.multiple_of(g * GROUP, GROUP)
                chunk = experts[:, pl.ds(h * HALF + at, GROUP), :].reshape(EXPERTS * GROUP, LANES)
                out = dot_nn(spread[b], chunk).astype(BF16)
                merged[h, b, :, pl.ds(at, GROUP), :] = out.reshape(SIDE * SIDE, GROUP, LANES)

            own = x if h == 0 else y
            side = y if h == 0 else x

            @pl.loop(0, SIDE)
            def _(t):
                q = (own + 1 + t) % SIDE
                for o in range(SIDE):
                    to = (side + o) % SIDE
                    slot = q * SIDE + to if h == 0 else to * SIDE + q
                    src = merged.at[h, b, slot]
                    dst = weights.at[h, SIDE * b + q, side]
                    if o == 0:
                        pltpu.make_async_copy(src, dst, m_recv.at[h, SIDE * b + q]).start()
                    else:
                        device = x * SIDE + to if h == 0 else to * SIDE + y
                        send(src, dst, m_send.at[h, b], m_recv.at[h, SIDE * b + q], (device, col))

    def joined(h, j, n):
        return jnp.concatenate(
            [weights[h, j, q, :, n * BLOCK:(n + 1) * BLOCK] for q in range(SIDE)], axis=1
        )

    def forward(b):
        own_half = pl.ds(pl.multiple_of(k * (SEG // 2), SEG // 2), SEG // 2)
        for o in range(SIDE - 1):
            for h in range(2):
                j = others(b, h)[o]
                drain(tokens.at[0, 0, :, 0:3 * PIECE], near_sem.at[h, j])
                part = tokens.at[h, j, :, own_half]
                send(part, part, pass_send.at[b], pass_sem.at[h, j], sibling)

        @pl.loop(0, 8)
        def _(i):
            t, h = i // 2, i % 2
            own = jnp.where(h == 0, x, y)
            q = (own + 1 + t) % SIDE
            j = SIDE * b + q
            drain(weights.at[h, j], m_recv.at[h, j])

            @pl.when(t < SIDE - 1)
            def _():
                drain(tokens.at[0, 0, :, 0:SEG // 2], pass_sem.at[h, j])

            @pl.when(t == SIDE - 1)
            def _():
                drain(tokens.at[h, j], tok_sem.at[h, j])

            for n in range(3):
                side = tokens[h, j, 0 if n < 2 else 1]
                part_out[h, j, n] = dot_nt(joined(h, j, n), side).astype(BF16)

            @pl.when(t < SIDE - 1)
            def _():
                send(
                    part_out.at[h, j], part_in.at[h, b, t], p_send.at[h, j], p_recv.at[h, b],
                    (line(h, q), col),
                )

    forward(0)
    forward(1)

    @pl.loop(0, 4)
    def _(i):
        b, h = i // 2, i % 2
        own = jnp.where(h == 0, x, y)
        j = SIDE * b + own
        drain(part_in.at[h, b], p_recv.at[h, b])

        def total(n):
            out = part_out[h, j, n].astype(F32)
            for o in range(SIDE - 1):
                out += part_in[h, b, o, n].astype(F32)
            return out

        gate, up, grad = total(0), total(1), total(2)
        sig = jax.nn.sigmoid(gate)
        gated = gate * sig
        deltas[h, j, 0] = (grad * up * sig * (1.0 + gate * (1.0 - sig))).astype(BF16)
        deltas[h, j, 1] = (grad * gated).astype(BF16)
        deltas[h, j, 2] = (gated * up).astype(BF16)
        for o in (1, SIDE - 1):
            send(
                deltas.at[h, j], deltas.at[h, j], d_send.at[h, b], d_recv.at[h, j],
                (line(h, (own + o) % SIDE), col),
            )

    @pl.loop(0, 4)
    def _(i):
        b, h = i // 2, i % 2
        own = jnp.where(h == 0, x, y)
        for n, o in ((1, 1), (0, SIDE - 1)):
            j = SIDE * b + (own + o) % SIDE
            drain(deltas.at[h, j], d_recv.at[h, j])
            part = deltas.at[h, j, :, :, pl.ds(n * BLOCK, BLOCK)]
            send(part, part, d_pass.at[h, b], d_recv.at[h, j], (line(h, (own - o + SIDE) % SIDE), col))

    def item(i):
        b, t, h = i // 8, (i // 2) % SIDE, i % 2
        own = jnp.where(h == 0, x, y)
        q = (own + jnp.where(t < 2, t, 5 - t)) % SIDE
        return b, t, h, q, SIDE * b + q

    def above(o):
        return (row, (z + o) % DEPTH * 2 + k)

    def pair_sum(i):
        b, t, h, q, j = item(i)
        drain(from_pair.at[h, j], s_recv.at[h, j])
        out = direct[i % 4, k].astype(F32) + from_pair[h, j].astype(F32)
        to_depth[h, j] = out.astype(BF16).reshape(DEPTH, CHUNK, WIDE)

        def hop(target, over, slot, sem):
            to = (z + target) % DEPTH
            send(to_depth.at[h, j, to], from_depth.at[h, j, slot], z_send.at[h, j], sem.at[h, j], above(over))

        hop(DEPTH - 3, DEPTH - 1, 4, z_pass)
        hop(3, 1, 5, z_pass)
        hop(4, DEPTH - 2, 6, z_pass)
        hop(1, 1, 0, z_recv)
        hop(DEPTH - 1, DEPTH - 1, 1, z_recv)

    def pass_sum(i):
        b, t, h, q, j = item(i)
        drain(from_depth.at[h, j, 4:7], z_pass.at[h, j])
        for o, slots, into in ((DEPTH - 2, (4, 6), 2), (2, (5,), 3)):
            to = (z + o) % DEPTH
            out = to_depth[h, j, to].astype(F32)
            for slot in slots:
                out += from_depth[h, j, slot].astype(F32)
            to_depth[h, j, to] = out.astype(BF16)
            send(to_depth.at[h, j, to], from_depth.at[h, j, into], z_send.at[h, j], z_recv.at[h, j], above(o))

    def send_terms(i):
        b, t, h, q, j = item(i)
        side = jnp.where(h == 0, y, x)
        slot = jnp.where(h == 0, q * SIDE + y, x * SIDE + q)
        for o in range(1, SIDE):
            to = (side + o) % SIDE
            send(
                weights.at[h, j, to], terms.at[h, b, slot], t_send.at[h, j], t_recv.at[h, b],
                (cross(h, to), col),
            )
        pltpu.make_async_copy(weights.at[h, j, side], terms.at[h, b, slot], t_recv.at[h, b]).start()

    def backward(i):
        b, t, h, q, j = item(i)

        @pl.when(t == SIDE - 1)
        def _():
            drain(deltas.at[h, j], d_recv.at[h, j])

        @pl.when(i >= 4)
        def _():
            drain(direct.at[0, 0], s_send.at[i % 4])

        both = deltas[h, j, 0:2].reshape(2 * HALF, SEG)
        out = dot_tn(both, jnp.concatenate([joined(h, j, 0), joined(h, j, 1)], axis=0))
        direct[i % 4] = out.astype(BF16).reshape(2, SEG // 2, WIDE)
        send(direct.at[i % 4, 1 - k], from_pair.at[h, j], s_send.at[i % 4], s_recv.at[h, j], sibling)

        for n in range(3):
            side = tokens[h, j, 0 if n < 2 else 1]
            out = dot_nn(deltas[h, j, n], side).astype(BF16)
            for p in range(SIDE):
                weights[h, j, p, :, n * BLOCK:(n + 1) * BLOCK] = out[:, p * BLOCK:(p + 1) * BLOCK]

        @pl.when(i > 0)
        def _():
            pair_sum(i - 1)

        @pl.when(i > 1)
        def _():
            pass_sum(i - 2)

    def depth_sums(b):
        @pl.loop(0, 8)
        def _(i):
            _, t, h, q, j = item(b * 8 + i)
            drain(from_depth.at[h, j, 0:4], z_recv.at[h, j])
            out = to_depth[h, j, z].astype(F32)
            for o in range(4):
                out += from_depth[h, j, o].astype(F32)
            depth_sum[h, j] = out.astype(BF16)
            own = jnp.where(h == 0, x, y)

            @pl.when(t == 0)
            def _():
                to_owner[h, b, own] = out.astype(BF16)

            @pl.when(t > 0)
            def _():
                send(
                    depth_sum.at[h, j], to_owner.at[h, b, own], o_send.at[h, b], o_recv.at[h, b],
                    (line(h, q), col),
                )

    def place(b, o=0):
        at = b * SEG + k * (SEG // 2) + (z + o) % DEPTH * CHUNK
        return direct_all.at[pl.ds(pl.multiple_of(at, CHUNK), CHUNK)]

    def half(b):
        return pl.ds(pl.multiple_of(b * SEG + k * (SEG // 2), SEG // 2), SEG // 2)

    def spread_direct(b):
        for h in range(2):
            drain(to_owner.at[h, b, 0:3], o_recv.at[h, b])
        pieces = []
        for p in range(SIDE):
            for q in range(SIDE):
                one = to_owner[0, b, p, :, q * BLOCK:(q + 1) * BLOCK].astype(F32)
                two = to_owner[1, b, q, :, p * BLOCK:(p + 1) * BLOCK].astype(F32)
                pieces.append((one + two).astype(BF16))
        place(b)[...] = jnp.concatenate(pieces, axis=1)
        for o in (1, DEPTH - 1):
            send(place(b), place(b), a_send.at[b], a_recv.at[b], above(o))
        for n, o in enumerate((2, DEPTH - 2)):
            send(place(b), place(b), a_send.at[b], a_pass.at[b, n], above(o))

    def pass_direct(b):
        for n, (back, steps) in enumerate(((DEPTH - 2, (1, 2)), (2, (DEPTH - 1,)))):
            drain(place(b, back), a_pass.at[b, n])
            for o in steps:
                send(place(b, back), place(b, back), a_send.at[b], a_recv.at[b], above(o))

    def share_direct(b):
        drain(direct_all.at[0:5 * CHUNK], a_recv.at[b])
        send(direct_all.at[half(b)], direct_all.at[half(b)], f_send.at[b], f_recv.at[b], sibling)

    def group(h, g):
        at = pl.multiple_of(g * GROUP, GROUP)
        return at, experts[:, pl.ds(h * HALF + at, GROUP), :].reshape(span, LANES)

    def products(b):
        inner[b] = jnp.zeros((span, span), F32)
        for h in range(2):
            drain(terms.at[h, b], t_recv.at[h, b])

            @pl.loop(0, HALF // GROUP, unroll=True)
            def _(g):
                at, chunk = group(h, g)
                term = terms[h, b, :, pl.ds(at, GROUP), :].reshape(span, LANES)
                inner[b] += dot_nt(term, chunk)

    def gradients(h):
        for b in range(2):
            drain(merged.at[h, b, 0:12], m_send.at[h, b])

        @pl.loop(0, HALF // GROUP, unroll=True)
        def _(g):
            at = pl.multiple_of(g * GROUP, GROUP)
            out = None
            for b in range(2):
                term = terms[h, b, :, pl.ds(at, GROUP), :].reshape(span, LANES)
                part = dot_nn(spread_t[b], term)
                out = part if out is None else out + part
            merged[h, 0, :, pl.ds(at, GROUP), :] = out.astype(BF16).reshape(EXPERTS, GROUP, LANES)

        for n, dst in enumerate((gate_out, up_out, down_out)):
            pltpu.make_async_copy(
                merged.at[h, 0, :, :, pl.ds(n * BLOCK, BLOCK)],
                dst.at[:, pl.ds(h * HALF, HALF), :], out_sem.at[h, n],
            ).start()

    @pl.loop(0, 12)
    def _(i):
        backward(i)
        send_terms(i)

    depth_sums(0)

    @pl.loop(12, 16)
    def _(i):
        backward(i)
        send_terms(i)

    pair_sum(15)
    pass_sum(14)
    pass_sum(15)
    spread_direct(0)
    depth_sums(1)
    products(0)
    pass_direct(0)
    spread_direct(1)
    products(1)

    fold = (iota((span, BLOCK), 0) // GROUP == iota((span, BLOCK), 1) % EXPERTS).astype(F32)
    here = iota((rows_all, BLOCK), 1) // EXPERTS == iota((rows_all, BLOCK), 0) % 8
    packed = []
    for b in range(2):
        kept = jnp.sum(jnp.where(same, inner[b], 0.0).reshape(EXPERTS, GROUP, span), axis=1)
        dense = lax.dot_general(
            kept, fold, (((1,), (0,)), ((), ())), precision=PRECISE, preferred_element_type=F32
        )
        packed.append(jnp.sum(jnp.where(here, dense, 0.0).reshape(2, 8, BLOCK), axis=1))
    packed.append(jnp.zeros((4, BLOCK), F32))
    in_row[0] = jnp.concatenate(packed, axis=0)

    @pl.loop(1, rows_all)
    def _(o):
        send(in_row.at[0], in_row.at[o], r_send, r_recv, ((row + o) % rows_all, col))

    pass_direct(1)
    share_direct(0)
    gradients(0)
    drain(in_row.at[1:rows_all], r_recv)

    @pl.loop(1, rows_all)
    def _(o):
        send(means.at[row], means.at[row], n_send, n_recv, ((row + o) % rows_all, col))

    out = in_row[0]
    for o in range(1, rows_all):
        out += in_row[o]
    in_col[0] = out

    @pl.loop(1, cols_all)
    def _(o):
        send(in_col.at[0], in_col.at[o], l_send, l_recv, (row, (col + o) % cols_all))

    gradients(1)
    share_direct(1)
    for b in range(2):
        drain(direct_all.at[0:SEG // 2], f_recv.at[b])
    copy = pltpu.make_async_copy(direct_all, direct_out, e_sem.at[0])
    copy.start()
    drain(in_col.at[1:cols_all], l_recv)
    out = in_col[0]
    for o in range(1, cols_all):
        out += in_col[o]
    wide = jnp.concatenate(
        [jnp.broadcast_to(out[p:p + 1, :], (8, BLOCK)) for p in range(4)], axis=0
    )
    shape = (2 * rows_all, BLOCK)
    wide = jnp.where(iota(shape, 1) // EXPERTS == iota(shape, 0) % 8, wide, 0.0)
    narrow = (iota((BLOCK, BLOCK), 0) % EXPERTS == iota((BLOCK, BLOCK), 1)).astype(F32)
    total = lax.dot_general(
        wide, narrow, (((1,), (0,)), ((), ())), precision=PRECISE, preferred_element_type=F32
    )
    logit_grad = routes[...] * (total - jnp.sum(routes[...] * total, axis=1, keepdims=True))
    source[...] = lax.dot_general(
        chooser[...], logit_grad, (((0,), (0,)), ((), ())),
        precision=PRECISE, preferred_element_type=F32,
    ).reshape(rows_all, 8, BLOCK)
    source_out[...] = source[...]
    drain(means.at[0:rows_all - 1], n_recv)
    means_out[...] = means[...]

    for h in range(2):
        for b in range(2):
            drain(deltas.at[h, 0:2], d_send.at[h, b])
            drain(deltas.at[h, 0], d_pass.at[h, b])
            drain(depth_sum.at[h, 0:3], o_send.at[h, b])
        own = x if h == 0 else y

        @pl.loop(0, 8)
        def _(j):
            @pl.when(j % SIDE != own)
            def _():
                drain(part_out.at[h, 0], p_send.at[h, j])

            drain(weights.at[h, 0, 0:3], t_send.at[h, j])
            drain(to_depth.at[h, 0, 0:7], z_send.at[h, j])

        for n in range(3):
            drain(merged.at[h, 0, :, :, pl.ds(n * BLOCK, BLOCK)], out_sem.at[h, n])
    for n in range(4):
        drain(direct.at[0, 0], s_send.at[n])
    drain(tokens.at[0, 0:3, 0], tok_send)
    drain(tokens.at[0, 0:3], near_send.at[0])
    drain(tokens.at[0, 0:3, 0], near_send.at[1])
    for b in range(2):
        drain(tokens.at[0, 0:3], pass_send.at[b])
        drain(direct_all.at[0:7 * CHUNK], a_send.at[b])
        drain(direct_all.at[0:SEG // 2], f_send.at[b])
    drain(scores.at[0:rows_all - 1], c_send)
    drain(means.at[0:rows_all - 1], n_send)
    drain(in_row.at[1:rows_all], r_send)
    drain(in_col.at[1:cols_all], l_send)
    copy.wait()


def moved(act, cot, gate_t, up_t, down, router_t, wanted):
    units = gate_t.shape[1]
    grad = jax.ShapeDtypeStruct((EXPERTS, units, BLOCK), BF16)
    vmem = pl.BlockSpec(memory_space=pltpu.VMEM)
    anywhere = pl.BlockSpec(memory_space=pl.ANY)
    dma = pltpu.SemaphoreType.DMA
    segs = SIDE * SIDE
    return pl.pallas_call(
        kernel,
        out_shape=(
            grad, grad, grad,
            jax.ShapeDtypeStruct((segs, 8, BLOCK), F32),
            jax.ShapeDtypeStruct((segs, 2 * segs, BLOCK), F32),
            jax.ShapeDtypeStruct((2 * SEG, 4 * WIDE), BF16),
        ),
        in_specs=[anywhere] * 5 + [vmem, pl.BlockSpec(memory_space=pltpu.SMEM)],
        out_specs=(anywhere, anywhere, anywhere, vmem, vmem, anywhere),
        scratch_shapes=[
            pltpu.VMEM((EXPERTS, 2 * HALF, LANES), BF16),
            pltpu.VMEM((2, 8, 2, SEG, WIDE), BF16),
            pltpu.VMEM((2, 2, segs, HALF, LANES), BF16),
            pltpu.VMEM((2, 8, SIDE, HALF, LANES), BF16),
            pltpu.VMEM((2, 2, segs, HALF, LANES), BF16),
            pltpu.VMEM((2, 8, 3, HALF, SEG), BF16),
            pltpu.VMEM((2, 2, 3, 3, HALF, SEG), BF16),
            pltpu.VMEM((2, 8, 3, HALF, SEG), BF16),
            pltpu.VMEM((4, 2, SEG // 2, WIDE), BF16),
            pltpu.VMEM((2, 8, SEG // 2, WIDE), BF16),
            pltpu.VMEM((2, 8, DEPTH, CHUNK, WIDE), BF16),
            pltpu.VMEM((2, 8, DEPTH - 1, CHUNK, WIDE), BF16),
            pltpu.VMEM((2, 8, CHUNK, WIDE), BF16),
            pltpu.VMEM((2, 2, SIDE, CHUNK, WIDE), BF16),
            pltpu.VMEM((2 * SEG, 4 * WIDE), BF16),
            pltpu.VMEM((2, EXPERTS * GROUP, EXPERTS * GROUP), F32),
            pltpu.VMEM((2, EXPERTS * GROUP, EXPERTS * GROUP), BF16),
            pltpu.VMEM((2, EXPERTS * GROUP, EXPERTS * GROUP), BF16),
            pltpu.VMEM((segs, 8, BLOCK), F32),
            pltpu.VMEM((segs, 2 * segs, BLOCK), F32),
            pltpu.VMEM((2 * segs, BLOCK), F32),
            pltpu.VMEM((segs, 8, BLOCK), F32),
            pltpu.VMEM((2 * DEPTH, 8, BLOCK), F32),
            pltpu.VMEM((segs, 8, BLOCK), F32),
            pltpu.VMEM((2 * segs, BLOCK), F32),
            dma((3,)), dma((2, 8)), dma, dma((2, 8)), dma((2,)), dma((2, 8)), dma((2,)),
            dma((2, 2)), dma((2, 8)), dma((2, 8)), dma((2, 2)), dma((2, 2)), dma((2, 8)), dma((2, 2)),
            dma((2, 8)), dma((2, 2)), dma((4,)), dma((2, 8)), dma((2, 8)), dma((2, 8)), dma((2, 8)),
            dma((2, 2)), dma((2, 2)), dma((2,)), dma((2,)), dma((2, 2)), dma((2,)), dma((2,)), dma((2, 3)),
            dma, dma, dma, dma, dma, dma, dma, dma,
        ],
        compiler_params=pltpu.CompilerParams(
            collective_id=1, has_side_effects=True, vmem_limit_bytes=63 * 2**20
        ),
        cost_estimate=pl.CostEstimate(flops=12 * 10**9, bytes_accessed=16 * 10**6, transcendentals=0),
        name="experts",
    )(act, cot, gate_t, up_t, down, router_t, wanted)


def finish_kernel(
    gate, up, down, direct, source, means, router_t,
    gate_out, up_out, down_out, input_out, router_out, grads, rows, in_sem, out_sem,
):
    parts = in_sem.shape[1]
    pairs = ((gate, gate_out), (up, up_out), (down, down_out))

    def pieces(n, p, size):
        at = pl.ds(p * (size // parts), size // parts)
        if n == 3:
            return direct.at[at], rows.at[at], input_out.at[at]
        return pairs[n][0].at[at], grads.at[n, at], pairs[n][1].at[at]

    sizes = [EXPERTS] * 3 + [rows.shape[0]]
    order = [(n, p) for p in range(parts) for n in (3, 0, 1, 2)]
    for n, p in order:
        src, mid, _ = pieces(n, p, sizes[n])
        pltpu.make_async_copy(src, mid, in_sem.at[n, p]).start()
    own = source[lax.axis_index("row")]
    mean_grad = lax.dot_general(
        own[:, 0:EXPERTS], router_t[...], (((1,), (0,)), ((), ())),
        precision=PRECISE, preferred_element_type=F32,
    ) / SEG
    for n, p in order:
        src, mid, dst = pieces(n, p, sizes[n])
        pltpu.make_async_copy(src, mid, in_sem.at[n, p]).wait()
        if n == 3:
            size = sizes[n] // parts
            extra = mean_grad[p * size // SEG:p * size // SEG + 1, :]

            @pl.loop(0, size // GROUP)
            def _(i):
                at = pl.ds(pl.multiple_of(p * size + i * GROUP, GROUP), GROUP)
                rows[at, :] = (rows[at, :].astype(F32) + extra).astype(BF16)

        pltpu.make_async_copy(mid, dst, out_sem.at[n, p]).start()
    segs = means.shape[0]
    for q in range(segs):
        out = None
        for b in range(2):
            part = lax.dot_general(
                source[:, b, :], means[:, b * segs + q, :], (((0,), (0,)), ((), ())),
                precision=PRECISE, preferred_element_type=F32,
            )
            out = part if out is None else out + part
        router_out[:, q * BLOCK:(q + 1) * BLOCK] = out[0:EXPERTS, :]
    for n, p in order:
        _, mid, dst = pieces(n, p, sizes[n])
        pltpu.make_async_copy(mid, dst, out_sem.at[n, p]).wait()


def finish(gate, up, down, direct, source, means, router_t):
    vmem = pl.BlockSpec(memory_space=pltpu.VMEM)
    anywhere = pl.BlockSpec(memory_space=pl.ANY)
    like = [jax.ShapeDtypeStruct(v.shape, v.dtype) for v in (gate, up, down, direct)]
    return pl.pallas_call(
        finish_kernel,
        out_shape=(*like, jax.ShapeDtypeStruct(router_t.shape, F32)),
        in_specs=[anywhere] * 4 + [vmem] * 3,
        out_specs=(anywhere,) * 4 + (vmem,),
        scratch_shapes=[
            pltpu.VMEM((3, *gate.shape), BF16),
            pltpu.VMEM(direct.shape, BF16),
            pltpu.SemaphoreType.DMA((4, 4)),
            pltpu.SemaphoreType.DMA((4, 4)),
        ],
        compiler_params=pltpu.CompilerParams(vmem_limit_bytes=60 * 2**20),
        name="finish",
    )(gate, up, down, direct, source, means, router_t)


def shards(activations, cotangent, router, gate_experts, up_experts, down_experts, route_source):
    router_t = router.T
    gate_t, up_t, down_t, source, means, direct = moved(
        activations, cotangent, gate_experts.transpose(0, 2, 1), up_experts.transpose(0, 2, 1),
        down_experts, router_t, route_source,
    )
    gate_t, up_t, down_t, input_grad, router_grad = finish(
        gate_t, up_t, down_t, direct, source, means, router_t
    )
    return (
        input_grad, gate_t.transpose(0, 2, 1), up_t.transpose(0, 2, 1), down_t, router_grad.T,
    )


def solution(mesh):
    in_specs = (
        P("row", None),
        P("row", None),
        P(),
        P(None, "row", "col"),
        P(None, "row", "col"),
        P(None, "col", "row"),
        P(),
    )
    out_specs = (
        P("row", None),
        P(None, "row", "col"),
        P(None, "row", "col"),
        P(None, "col", "row"),
        P(),
    )
    return jax.shard_map(shards, mesh=mesh, in_specs=in_specs, out_specs=out_specs, check_vma=False)
```

```python
import functools

import jax
import jax.numpy as jnp
from jax import lax
from jax.experimental import pallas as pl
from jax.experimental.pallas import tpu as pltpu
from jax.sharding import PartitionSpec as P

SEG = 256
EXPERTS = 16
SIDE = 4
DEPTH = 8
BLOCK = 128
HALF = 176
LANES = 3 * BLOCK
WIDE = SIDE * BLOCK
GROUP = 16
CHUNK = 16
PIECE = 32
PRECISE = lax.Precision.HIGHEST
MESH = pl.DeviceIdType.MESH
F32 = jnp.float32
BF16 = jnp.bfloat16


def dot_nn(a, b):
    return lax.dot_general(a, b, (((1,), (0,)), ((), ())), preferred_element_type=F32)


def dot_nt(a, b):
    return lax.dot_general(a, b, (((1,), (1,)), ((), ())), preferred_element_type=F32)


def dot_tn(a, b):
    return lax.dot_general(a, b, (((0,), (0,)), ((), ())), preferred_element_type=F32)


def drain(ref, sem):
    pltpu.make_async_copy(ref, ref, sem).wait()


def kernel(
    act, cot, gate_t, up_t, down, router_t, wanted,
    gate_out, up_out, down_out, source_out, means_out, direct_out,
    experts, tokens, merged, weights, terms, part_out, part_mid, part_in, deltas,
    direct, from_pair, to_depth, from_depth, depth_sum, to_owner, direct_all, inner,
    spread, spread_t, scores, means, routes, in_row, in_col, source, chooser,
    e_sem, tok_sem, tok_send, near_sem, near_send, pass_sem, pass_send, m_send, m_recv, p_send, mid_recv, p_recv, d_send, d_recv, d_pass,
    t_send, t_recv, s_send, s_recv, z_send, z_recv, z_pass, o_send, o_recv, a_send, a_recv, a_pass,
    f_send, f_recv, out_sem, c_send, c_recv, n_send, n_recv, r_send, r_recv, l_send, l_recv,
):
    row = lax.axis_index("row")
    col = lax.axis_index("col")
    x, y = row // SIDE, row % SIDE
    z, k = col // 2, col % 2
    sibling = (row, z * 2 + 1 - k)

    def line(h, at):
        return jnp.where(h == 0, at * SIDE + y, x * SIDE + at)

    def cross(h, at):
        return jnp.where(h == 0, x * SIDE + at, at * SIDE + y)

    def nth(t):
        return jnp.where(t == 0, 2, jnp.where(t == 1, 1, jnp.where(t == 2, 3, 0)))

    def send(src, dst, send_sem, recv_sem, to):
        pltpu.make_async_remote_copy(
            src_ref=src, dst_ref=dst, send_sem=send_sem, recv_sem=recv_sem,
            device_id=to, device_id_type=MESH,
        ).start()

    loads = [
        pltpu.make_async_copy(src, experts.at[:, :, pl.ds(n * BLOCK, BLOCK)], e_sem.at[n])
        for n, src in enumerate((gate_t, up_t, down))
    ]
    read = pltpu.make_async_copy(act, direct_all, out_sem.at[0, 0])
    read.start()
    for load in loads:
        load.start()

    rows_all = SIDE * SIDE
    cols_all = 2 * DEPTH
    barrier = pltpu.get_barrier_semaphore()

    @pl.loop(1, rows_all)
    def _(o):
        pl.semaphore_signal(
            barrier, inc=1, device_id=((row + o) % rows_all, col), device_id_type=MESH
        )

    @pl.loop(1, cols_all)
    def _(o):
        pl.semaphore_signal(
            barrier, inc=1, device_id=(row, (col + o) % cols_all), device_id_type=MESH
        )

    read.wait()
    found = []
    for b in range(2):
        def add(i, total):
            at = pl.multiple_of(b * SEG + i * GROUP, GROUP)
            return total + direct_all[pl.ds(at, GROUP), :].astype(F32)

        total = lax.fori_loop(0, SEG // GROUP, add, jnp.zeros((GROUP, 4 * WIDE), F32))
        found.append(jnp.sum(total, axis=0, keepdims=True) / SEG)
        for q in range(rows_all):
            means[row, b * rows_all + q:b * rows_all + q + 1, :] = found[b][:, q * BLOCK:(q + 1) * BLOCK]
    found.append(jnp.zeros((6, 4 * WIDE), F32))
    scores[row] = jnp.zeros((8, BLOCK), F32)
    scores[row, :, 0:EXPERTS] = lax.dot_general(
        jnp.concatenate(found, axis=0), router_t[...], (((1,), (1,)), ((), ())),
        precision=PRECISE, preferred_element_type=F32,
    )
    pl.semaphore_wait(barrier, rows_all + cols_all - 2)

    @pl.loop(1, rows_all)
    def _(o):
        send(scores.at[row], scores.at[row], c_send, c_recv, ((row + o) % rows_all, col))

    first = pl.multiple_of((k * SIDE + z % SIDE) * PIECE, PIECE)
    piece = pl.ds(first, PIECE)

    @pl.loop(0, 2)
    def _(b):
        rows = pl.ds(pl.multiple_of(b * SEG + first, PIECE), PIECE)
        for o in range(1, SIDE):
            for n, src in enumerate((act, cot)):
                to = (x + o) % SIDE
                j = SIDE * b + x
                send(
                    src.at[rows, pl.ds(pl.multiple_of(to * WIDE, WIDE), WIDE)],
                    tokens.at[0, j, n, piece], tok_send, tok_sem.at[0, j], (to * SIDE + y, col),
                )
                to = (y + o) % SIDE
                j = SIDE * b + y
                for q in range(SIDE):
                    send(
                        src.at[rows, pl.ds(pl.multiple_of((q * SIDE + to) * BLOCK, BLOCK), BLOCK)],
                        tokens.at[1, j, n, piece, pl.ds(q * BLOCK, BLOCK)],
                        tok_send, tok_sem.at[1, j], (x * SIDE + to, col),
                    )

    for b in range(2):
        rows = pl.ds(b * SEG, SEG)
        for n, src in enumerate((act, cot)):
            pltpu.make_async_copy(
                src.at[rows, pl.ds(pl.multiple_of(x * WIDE, WIDE), WIDE)],
                tokens.at[0, SIDE * b + x, n], tok_sem.at[0, SIDE * b + x],
            ).start()
            for q in range(SIDE):
                pltpu.make_async_copy(
                    src.at[rows, pl.ds(pl.multiple_of((q * SIDE + y) * BLOCK, BLOCK), BLOCK)],
                    tokens.at[1, SIDE * b + y, n, :, pl.ds(q * BLOCK, BLOCK)],
                    tok_sem.at[1, SIDE * b + y],
                ).start()
    for s in range(2 * rows_all):
        at = (s % 2) * rows_all + s // 2
        v = wanted[s]
        place = (v // 2) * 8 + v % 2
        lanes = lax.broadcasted_iota(jnp.int32, (1, BLOCK), 1)
        chooser[at:at + 1, :] = jnp.where(lanes == place, 1.0, 0.0).astype(F32)

    drain(scores.at[0:rows_all - 1], c_recv)
    logits = lax.dot_general(
        chooser[...], scores[...].reshape(rows_all * 8, BLOCK), (((1,), (0,)), ((), ())),
        precision=PRECISE, preferred_element_type=F32,
    )
    real = lax.broadcasted_iota(jnp.int32, logits.shape, 1) < EXPERTS
    powers = jnp.where(real, jnp.exp(logits), 0.0)
    routes[...] = powers / jnp.sum(powers, axis=1, keepdims=True)
    span = EXPERTS * GROUP

    def iota(shape, axis):
        return lax.broadcasted_iota(jnp.int32, shape, axis)

    same = iota((span, span), 0) % GROUP == iota((span, span), 1) % GROUP
    pick = (iota((span, rows_all), 0) // GROUP == iota((span, rows_all), 1)).astype(BF16)
    expand = (iota((span, BLOCK), 0) // GROUP == iota((span, BLOCK), 1)).astype(BF16)
    for b in range(2):
        rounded = routes[b * rows_all:(b + 1) * rows_all, :].astype(BF16)
        long = dot_nt(dot_nn(pick, rounded).astype(BF16), expand)
        spread[b] = jnp.where(same, long, 0.0).astype(BF16)
        long = dot_nt(dot_nt(expand, rounded).astype(BF16), pick)
        spread_t[b] = jnp.where(same, long, 0.0).astype(BF16)

    def others(b, h):
        own = x if h == 0 else y
        return [SIDE * b + (own + o) % SIDE for o in range(1, SIDE)]

    for b in range(2):
        for o in range(SIDE - 1):
            for h in range(2):
                j = others(b, h)[o]
                drain(tokens.at[0, 0, :, 0:PIECE], tok_sem.at[h, j])
                both = tokens.at[h, j, :, piece]
                for step in (1, DEPTH - 1):
                    to = (row, (z + step) % DEPTH * 2 + k)
                    send(both, both, near_send.at[0], near_sem.at[h, j], to)
                for n, step in enumerate((2, DEPTH - 2)):
                    one = tokens.at[h, j, n, piece]
                    to = (row, (z + step) % DEPTH * 2 + k)
                    send(one, one, near_send.at[1], near_sem.at[h, j], to)
    for load in loads:
        load.wait()

    for b in range(2):
        for h in range(2):

            @pl.loop(0, HALF // GROUP)
            def _(g):
                at = pl.multiple_of(g * GROUP, GROUP)
                chunk = experts[:, pl.ds(h * HALF + at, GROUP), :].reshape(EXPERTS * GROUP, LANES)
                out = dot_nn(spread[b], chunk).astype(BF16)
                merged[h, b, :, pl.ds(at, GROUP), :] = out.reshape(SIDE * SIDE, GROUP, LANES)

            own = x if h == 0 else y
            side = y if h == 0 else x

            @pl.loop(0, SIDE)
            def _(t):
                q = (own + nth(t)) % SIDE
                for o in range(SIDE):
                    to = (side + o) % SIDE
                    slot = q * SIDE + to if h == 0 else to * SIDE + q
                    src = merged.at[h, b, slot]
                    dst = weights.at[h, SIDE * b + q, side]
                    if o == 0:
                        pltpu.make_async_copy(src, dst, m_recv.at[h, SIDE * b + q]).start()
                    else:
                        device = x * SIDE + to if h == 0 else to * SIDE + y
                        send(src, dst, m_send.at[h, b], m_recv.at[h, SIDE * b + q], (device, col))

    def joined(h, j, n):
        return jnp.concatenate(
            [weights[h, j, q, :, n * BLOCK:(n + 1) * BLOCK] for q in range(SIDE)], axis=1
        )

    def forward(b):
        own_half = pl.ds(pl.multiple_of(k * (SEG // 2), SEG // 2), SEG // 2)
        for o in range(SIDE - 1):
            for h in range(2):
                j = others(b, h)[o]
                drain(tokens.at[0, 0, :, 0:3 * PIECE], near_sem.at[h, j])
                part = tokens.at[h, j, :, own_half]
                send(part, part, pass_send.at[b], pass_sem.at[h, j], sibling)

        @pl.loop(0, 8)
        def _(i):
            t, h = i // 2, i % 2
            own = jnp.where(h == 0, x, y)
            q = (own + nth(t)) % SIDE
            j = SIDE * b + q
            drain(weights.at[h, j], m_recv.at[h, j])

            @pl.when(t < SIDE - 1)
            def _():
                drain(tokens.at[0, 0, :, 0:SEG // 2], pass_sem.at[h, j])

            @pl.when(t == SIDE - 1)
            def _():
                drain(tokens.at[h, j], tok_sem.at[h, j])

            for n in range(3):
                side = tokens[h, j, 0 if n < 2 else 1]
                part_out[h, j, n] = dot_nt(joined(h, j, n), side).astype(BF16)

            @pl.when(t == 0)
            def _():
                for n, o in enumerate((SIDE - 1, 1)):
                    send(
                        part_out.at[h, j, :, :, pl.ds(n * BLOCK, BLOCK)], part_mid.at[h, b, n],
                        p_send.at[h, j], mid_recv.at[h, b, n], (line(h, (own + o) % SIDE), col),
                    )

    forward(0)
    forward(1)

    @pl.loop(0, 4)
    def _(i):
        b, h = i // 2, i % 2
        own = jnp.where(h == 0, x, y)
        for t, o in enumerate((1, SIDE - 1)):
            n = 1 - t
            q = (own + o) % SIDE
            j = SIDE * b + q
            lanes = slice(n * BLOCK, (n + 1) * BLOCK)
            drain(part_mid.at[h, b, n], mid_recv.at[h, b, n])
            for m in range(3):
                both = part_out[h, j, m, :, lanes].astype(F32) + part_mid[h, b, n, m].astype(F32)
                part_out[h, j, m, :, lanes] = both.astype(BF16)
            send(part_out.at[h, j], part_in.at[h, b, t], p_send.at[h, j], p_recv.at[h, b], (line(h, q), col))

    @pl.loop(0, 4)
    def _(i):
        b, h = i // 2, i % 2
        own = jnp.where(h == 0, x, y)
        j = SIDE * b + own
        drain(part_in.at[h, b], p_recv.at[h, b])

        def total(n):
            out = part_out[h, j, n].astype(F32)
            for o in range(2):
                out += part_in[h, b, o, n].astype(F32)
            return out

        gate, up, grad = total(0), total(1), total(2)
        sig = jax.nn.sigmoid(gate)
        gated = gate * sig
        deltas[h, j, 0] = (grad * up * sig * (1.0 + gate * (1.0 - sig))).astype(BF16)
        deltas[h, j, 1] = (grad * gated).astype(BF16)
        deltas[h, j, 2] = (gated * up).astype(BF16)
        for o in (1, SIDE - 1):
            send(
                deltas.at[h, j], deltas.at[h, j], d_send.at[h, b], d_recv.at[h, j],
                (line(h, (own + o) % SIDE), col),
            )

    @pl.loop(0, 4)
    def _(i):
        b, h = i // 2, i % 2
        own = jnp.where(h == 0, x, y)
        for n, o in ((1, 1), (0, SIDE - 1)):
            j = SIDE * b + (own + o) % SIDE
            drain(deltas.at[h, j], d_recv.at[h, j])
            part = deltas.at[h, j, :, :, pl.ds(n * BLOCK, BLOCK)]
            send(part, part, d_pass.at[h, b], d_recv.at[h, j], (line(h, (own - o + SIDE) % SIDE), col))

    def item(i):
        b, t, h = i // 8, (i // 2) % SIDE, i % 2
        own = jnp.where(h == 0, x, y)
        q = (own + jnp.where(t < 2, t, 5 - t)) % SIDE
        return b, t, h, q, SIDE * b + q

    def above(o):
        return (row, (z + o) % DEPTH * 2 + k)

    def pair_sum(i):
        b, t, h, q, j = item(i)
        drain(from_pair.at[h, j], s_recv.at[h, j])
        out = direct[i % 4, k].astype(F32) + from_pair[h, j].astype(F32)
        to_depth[h, j] = out.astype(BF16).reshape(DEPTH, CHUNK, WIDE)

        def hop(target, over, slot, sem):
            to = (z + target) % DEPTH
            send(to_depth.at[h, j, to], from_depth.at[h, j, slot], z_send.at[h, j], sem.at[h, j], above(over))

        hop(DEPTH - 3, DEPTH - 1, 4, z_pass)
        hop(3, 1, 5, z_pass)
        hop(4, DEPTH - 2, 6, z_pass)
        hop(1, 1, 0, z_recv)
        hop(DEPTH - 1, DEPTH - 1, 1, z_recv)

    def pass_sum(i):
        b, t, h, q, j = item(i)
        drain(from_depth.at[h, j, 4:7], z_pass.at[h, j])
        for o, slots, into in ((DEPTH - 2, (4, 6), 2), (2, (5,), 3)):
            to = (z + o) % DEPTH
            out = to_depth[h, j, to].astype(F32)
            for slot in slots:
                out += from_depth[h, j, slot].astype(F32)
            to_depth[h, j, to] = out.astype(BF16)
            send(to_depth.at[h, j, to], from_depth.at[h, j, into], z_send.at[h, j], z_recv.at[h, j], above(o))

    def send_terms(i):
        b, t, h, q, j = item(i)
        side = jnp.where(h == 0, y, x)
        slot = jnp.where(h == 0, q * SIDE + y, x * SIDE + q)
        for o in range(1, SIDE):
            to = (side + o) % SIDE
            send(
                weights.at[h, j, to], terms.at[h, b, slot], t_send.at[h, j], t_recv.at[h, b],
                (cross(h, to), col),
            )
        pltpu.make_async_copy(weights.at[h, j, side], terms.at[h, b, slot], t_recv.at[h, b]).start()

    def backward(i):
        b, t, h, q, j = item(i)

        @pl.when(t == SIDE - 1)
        def _():
            drain(deltas.at[h, j], d_recv.at[h, j])

        @pl.when(i >= 4)
        def _():
            drain(direct.at[0, 0], s_send.at[i % 4])

        both = deltas[h, j, 0:2].reshape(2 * HALF, SEG)
        out = dot_tn(both, jnp.concatenate([joined(h, j, 0), joined(h, j, 1)], axis=0))
        direct[i % 4] = out.astype(BF16).reshape(2, SEG // 2, WIDE)
        send(direct.at[i % 4, 1 - k], from_pair.at[h, j], s_send.at[i % 4], s_recv.at[h, j], sibling)

        for n in range(3):
            side = tokens[h, j, 0 if n < 2 else 1]
            out = dot_nn(deltas[h, j, n], side).astype(BF16)
            for p in range(SIDE):
                weights[h, j, p, :, n * BLOCK:(n + 1) * BLOCK] = out[:, p * BLOCK:(p + 1) * BLOCK]

        @pl.when(i > 0)
        def _():
            pair_sum(i - 1)

        @pl.when(i > 1)
        def _():
            pass_sum(i - 2)

    def depth_sums(b):
        @pl.loop(0, 8)
        def _(i):
            _, t, h, q, j = item(b * 8 + i)
            drain(from_depth.at[h, j, 0:4], z_recv.at[h, j])
            out = to_depth[h, j, z].astype(F32)
            for o in range(4):
                out += from_depth[h, j, o].astype(F32)
            depth_sum[h, j] = out.astype(BF16)
            own = jnp.where(h == 0, x, y)

            @pl.when(t == 0)
            def _():
                to_owner[h, b, own] = out.astype(BF16)

            @pl.when(t > 0)
            def _():
                send(
                    depth_sum.at[h, j], to_owner.at[h, b, own], o_send.at[h, b], o_recv.at[h, b],
                    (line(h, q), col),
                )

    def place(b, o=0):
        at = b * SEG + k * (SEG // 2) + (z + o) % DEPTH * CHUNK
        return direct_all.at[pl.ds(pl.multiple_of(at, CHUNK), CHUNK)]

    def half(b):
        return pl.ds(pl.multiple_of(b * SEG + k * (SEG // 2), SEG // 2), SEG // 2)

    def spread_direct(b):
        for h in range(2):
            drain(to_owner.at[h, b, 0:3], o_recv.at[h, b])
        pieces = []
        for p in range(SIDE):
            for q in range(SIDE):
                one = to_owner[0, b, p, :, q * BLOCK:(q + 1) * BLOCK].astype(F32)
                two = to_owner[1, b, q, :, p * BLOCK:(p + 1) * BLOCK].astype(F32)
                pieces.append((one + two).astype(BF16))
        place(b)[...] = jnp.concatenate(pieces, axis=1)
        for o in (1, DEPTH - 1):
            send(place(b), place(b), a_send.at[b], a_recv.at[b], above(o))
        for n, o in enumerate((2, DEPTH - 2)):
            send(place(b), place(b), a_send.at[b], a_pass.at[b, n], above(o))

    def pass_direct(b):
        for n, (back, steps) in enumerate(((DEPTH - 2, (1, 2)), (2, (DEPTH - 1,)))):
            drain(place(b, back), a_pass.at[b, n])
            for o in steps:
                send(place(b, back), place(b, back), a_send.at[b], a_recv.at[b], above(o))

    def share_direct(b):
        drain(direct_all.at[0:5 * CHUNK], a_recv.at[b])
        send(direct_all.at[half(b)], direct_all.at[half(b)], f_send.at[b], f_recv.at[b], sibling)

    def group(h, g):
        at = pl.multiple_of(g * GROUP, GROUP)
        return at, experts[:, pl.ds(h * HALF + at, GROUP), :].reshape(span, LANES)

    def products(b):
        inner[b] = jnp.zeros((span, span), F32)
        for h in range(2):
            drain(terms.at[h, b], t_recv.at[h, b])

            @pl.loop(0, HALF // GROUP, unroll=True)
            def _(g):
                at, chunk = group(h, g)
                term = terms[h, b, :, pl.ds(at, GROUP), :].reshape(span, LANES)
                inner[b] += dot_nt(term, chunk)

    def gradients(h):
        for b in range(2):
            drain(merged.at[h, b, 0:12], m_send.at[h, b])

        @pl.loop(0, HALF // GROUP, unroll=True)
        def _(g):
            at = pl.multiple_of(g * GROUP, GROUP)
            out = None
            for b in range(2):
                term = terms[h, b, :, pl.ds(at, GROUP), :].reshape(span, LANES)
                part = dot_nn(spread_t[b], term)
                out = part if out is None else out + part
            merged[h, 0, :, pl.ds(at, GROUP), :] = out.astype(BF16).reshape(EXPERTS, GROUP, LANES)

        for n, dst in enumerate((gate_out, up_out, down_out)):
            pltpu.make_async_copy(
                merged.at[h, 0, :, :, pl.ds(n * BLOCK, BLOCK)],
                dst.at[:, pl.ds(h * HALF, HALF), :], out_sem.at[h, n],
            ).start()

    @pl.loop(0, 12)
    def _(i):
        backward(i)
        send_terms(i)

    depth_sums(0)

    @pl.loop(12, 16)
    def _(i):
        backward(i)
        send_terms(i)

    pair_sum(15)
    pass_sum(14)
    pass_sum(15)
    spread_direct(0)
    depth_sums(1)
    products(0)
    pass_direct(0)
    spread_direct(1)
    products(1)

    fold = (iota((span, BLOCK), 0) // GROUP == iota((span, BLOCK), 1) % EXPERTS).astype(F32)
    here = iota((rows_all, BLOCK), 1) // EXPERTS == iota((rows_all, BLOCK), 0) % 8
    packed = []
    for b in range(2):
        kept = jnp.sum(jnp.where(same, inner[b], 0.0).reshape(EXPERTS, GROUP, span), axis=1)
        dense = lax.dot_general(
            kept, fold, (((1,), (0,)), ((), ())), precision=PRECISE, preferred_element_type=F32
        )
        packed.append(jnp.sum(jnp.where(here, dense, 0.0).reshape(2, 8, BLOCK), axis=1))
    packed.append(jnp.zeros((4, BLOCK), F32))
    in_row[0] = jnp.concatenate(packed, axis=0)

    @pl.loop(1, rows_all)
    def _(o):
        send(in_row.at[0], in_row.at[o], r_send, r_recv, ((row + o) % rows_all, col))

    pass_direct(1)
    share_direct(0)
    gradients(0)
    drain(in_row.at[1:rows_all], r_recv)

    @pl.loop(1, rows_all)
    def _(o):
        send(means.at[row], means.at[row], n_send, n_recv, ((row + o) % rows_all, col))

    out = in_row[0]
    for o in range(1, rows_all):
        out += in_row[o]
    in_col[0] = out

    @pl.loop(1, cols_all)
    def _(o):
        send(in_col.at[0], in_col.at[o], l_send, l_recv, (row, (col + o) % cols_all))

    gradients(1)
    share_direct(1)
    for b in range(2):
        drain(direct_all.at[0:SEG // 2], f_recv.at[b])
    copy = pltpu.make_async_copy(direct_all, direct_out, e_sem.at[0])
    copy.start()
    drain(in_col.at[1:cols_all], l_recv)
    out = in_col[0]
    for o in range(1, cols_all):
        out += in_col[o]
    wide = jnp.concatenate(
        [jnp.broadcast_to(out[p:p + 1, :], (8, BLOCK)) for p in range(4)], axis=0
    )
    shape = (2 * rows_all, BLOCK)
    wide = jnp.where(iota(shape, 1) // EXPERTS == iota(shape, 0) % 8, wide, 0.0)
    narrow = (iota((BLOCK, BLOCK), 0) % EXPERTS == iota((BLOCK, BLOCK), 1)).astype(F32)
    total = lax.dot_general(
        wide, narrow, (((1,), (0,)), ((), ())), precision=PRECISE, preferred_element_type=F32
    )
    logit_grad = routes[...] * (total - jnp.sum(routes[...] * total, axis=1, keepdims=True))
    source[...] = lax.dot_general(
        chooser[...], logit_grad, (((0,), (0,)), ((), ())),
        precision=PRECISE, preferred_element_type=F32,
    ).reshape(rows_all, 8, BLOCK)
    source_out[...] = source[...]
    drain(means.at[0:rows_all - 1], n_recv)
    means_out[...] = means[...]

    for h in range(2):
        for b in range(2):
            drain(deltas.at[h, 0:2], d_send.at[h, b])
            drain(deltas.at[h, 0], d_pass.at[h, b])
            drain(depth_sum.at[h, 0:3], o_send.at[h, b])
        own = x if h == 0 else y

        @pl.loop(0, 8)
        def _(j):
            @pl.when(j % SIDE != own)
            def _():
                drain(part_out.at[h, 0], p_send.at[h, j])

            drain(weights.at[h, 0, 0:3], t_send.at[h, j])
            drain(to_depth.at[h, 0, 0:7], z_send.at[h, j])

        for n in range(3):
            drain(merged.at[h, 0, :, :, pl.ds(n * BLOCK, BLOCK)], out_sem.at[h, n])
    for n in range(4):
        drain(direct.at[0, 0], s_send.at[n])
    drain(tokens.at[0, 0:3, 0], tok_send)
    drain(tokens.at[0, 0:3], near_send.at[0])
    drain(tokens.at[0, 0:3, 0], near_send.at[1])
    for b in range(2):
        drain(tokens.at[0, 0:3], pass_send.at[b])
        drain(direct_all.at[0:7 * CHUNK], a_send.at[b])
        drain(direct_all.at[0:SEG // 2], f_send.at[b])
    drain(scores.at[0:rows_all - 1], c_send)
    drain(means.at[0:rows_all - 1], n_send)
    drain(in_row.at[1:rows_all], r_send)
    drain(in_col.at[1:cols_all], l_send)
    copy.wait()


def moved(act, cot, gate_t, up_t, down, router_t, wanted):
    units = gate_t.shape[1]
    grad = jax.ShapeDtypeStruct((EXPERTS, units, BLOCK), BF16)
    vmem = pl.BlockSpec(memory_space=pltpu.VMEM)
    anywhere = pl.BlockSpec(memory_space=pl.ANY)
    dma = pltpu.SemaphoreType.DMA
    segs = SIDE * SIDE
    return pl.pallas_call(
        kernel,
        out_shape=(
            grad, grad, grad,
            jax.ShapeDtypeStruct((segs, 8, BLOCK), F32),
            jax.ShapeDtypeStruct((segs, 2 * segs, BLOCK), F32),
            jax.ShapeDtypeStruct((2 * SEG, 4 * WIDE), BF16),
        ),
        in_specs=[anywhere] * 5 + [vmem, pl.BlockSpec(memory_space=pltpu.SMEM)],
        out_specs=(anywhere, anywhere, anywhere, vmem, vmem, anywhere),
        scratch_shapes=[
            pltpu.VMEM((EXPERTS, 2 * HALF, LANES), BF16),
            pltpu.VMEM((2, 8, 2, SEG, WIDE), BF16),
            pltpu.VMEM((2, 2, segs, HALF, LANES), BF16),
            pltpu.VMEM((2, 8, SIDE, HALF, LANES), BF16),
            pltpu.VMEM((2, 2, segs, HALF, LANES), BF16),
            pltpu.VMEM((2, 8, 3, HALF, SEG), BF16),
            pltpu.VMEM((2, 2, 2, 3, HALF, BLOCK), BF16),
            pltpu.VMEM((2, 2, 2, 3, HALF, SEG), BF16),
            pltpu.VMEM((2, 8, 3, HALF, SEG), BF16),
            pltpu.VMEM((4, 2, SEG // 2, WIDE), BF16),
            pltpu.VMEM((2, 8, SEG // 2, WIDE), BF16),
            pltpu.VMEM((2, 8, DEPTH, CHUNK, WIDE), BF16),
            pltpu.VMEM((2, 8, DEPTH - 1, CHUNK, WIDE), BF16),
            pltpu.VMEM((2, 8, CHUNK, WIDE), BF16),
            pltpu.VMEM((2, 2, SIDE, CHUNK, WIDE), BF16),
            pltpu.VMEM((2 * SEG, 4 * WIDE), BF16),
            pltpu.VMEM((2, EXPERTS * GROUP, EXPERTS * GROUP), F32),
            pltpu.VMEM((2, EXPERTS * GROUP, EXPERTS * GROUP), BF16),
            pltpu.VMEM((2, EXPERTS * GROUP, EXPERTS * GROUP), BF16),
            pltpu.VMEM((segs, 8, BLOCK), F32),
            pltpu.VMEM((segs, 2 * segs, BLOCK), F32),
            pltpu.VMEM((2 * segs, BLOCK), F32),
            pltpu.VMEM((segs, 8, BLOCK), F32),
            pltpu.VMEM((2 * DEPTH, 8, BLOCK), F32),
            pltpu.VMEM((segs, 8, BLOCK), F32),
            pltpu.VMEM((2 * segs, BLOCK), F32),
            dma((3,)), dma((2, 8)), dma, dma((2, 8)), dma((2,)), dma((2, 8)), dma((2,)),
            dma((2, 2)), dma((2, 8)), dma((2, 8)), dma((2, 2, 2)), dma((2, 2)), dma((2, 2)), dma((2, 8)), dma((2, 2)),
            dma((2, 8)), dma((2, 2)), dma((4,)), dma((2, 8)), dma((2, 8)), dma((2, 8)), dma((2, 8)),
            dma((2, 2)), dma((2, 2)), dma((2,)), dma((2,)), dma((2, 2)), dma((2,)), dma((2,)), dma((2, 3)),
            dma, dma, dma, dma, dma, dma, dma, dma,
        ],
        compiler_params=pltpu.CompilerParams(
            collective_id=1, has_side_effects=True, vmem_limit_bytes=63 * 2**20
        ),
        cost_estimate=pl.CostEstimate(flops=12 * 10**9, bytes_accessed=16 * 10**6, transcendentals=0),
        name="experts",
    )(act, cot, gate_t, up_t, down, router_t, wanted)


def finish_kernel(
    gate, up, down, direct, source, means, router_t,
    gate_out, up_out, down_out, input_out, router_out, grads, rows, in_sem, out_sem,
):
    parts = in_sem.shape[1]
    pairs = ((gate, gate_out), (up, up_out), (down, down_out))

    def pieces(n, p, size):
        at = pl.ds(p * (size // parts), size // parts)
        if n == 3:
            return direct.at[at], rows.at[at], input_out.at[at]
        return pairs[n][0].at[at], grads.at[n, at], pairs[n][1].at[at]

    sizes = [EXPERTS] * 3 + [rows.shape[0]]
    order = [(n, p) for p in range(parts) for n in (3, 0, 1, 2)]
    for n, p in order:
        src, mid, _ = pieces(n, p, sizes[n])
        pltpu.make_async_copy(src, mid, in_sem.at[n, p]).start()
    own = source[lax.axis_index("row")]
    mean_grad = lax.dot_general(
        own[:, 0:EXPERTS], router_t[...], (((1,), (0,)), ((), ())),
        precision=PRECISE, preferred_element_type=F32,
    ) / SEG
    for n, p in order:
        src, mid, dst = pieces(n, p, sizes[n])
        pltpu.make_async_copy(src, mid, in_sem.at[n, p]).wait()
        if n == 3:
            size = sizes[n] // parts
            extra = mean_grad[p * size // SEG:p * size // SEG + 1, :]

            @pl.loop(0, size // GROUP)
            def _(i):
                at = pl.ds(pl.multiple_of(p * size + i * GROUP, GROUP), GROUP)
                rows[at, :] = (rows[at, :].astype(F32) + extra).astype(BF16)

        pltpu.make_async_copy(mid, dst, out_sem.at[n, p]).start()
    segs = means.shape[0]
    out = None
    for b in range(2):
        rows_b = jnp.concatenate([means[:, b * segs + q, :] for q in range(segs)], axis=1)
        part = lax.dot_general(
            source[:, b, 0:EXPERTS], rows_b, (((0,), (0,)), ((), ())),
            precision=PRECISE, preferred_element_type=F32,
        )
        out = part if out is None else out + part
    router_out[...] = out
    for n, p in order:
        _, mid, dst = pieces(n, p, sizes[n])
        pltpu.make_async_copy(mid, dst, out_sem.at[n, p]).wait()


def finish(gate, up, down, direct, source, means, router_t):
    vmem = pl.BlockSpec(memory_space=pltpu.VMEM)
    anywhere = pl.BlockSpec(memory_space=pl.ANY)
    like = [jax.ShapeDtypeStruct(v.shape, v.dtype) for v in (gate, up, down, direct)]
    return pl.pallas_call(
        finish_kernel,
        out_shape=(*like, jax.ShapeDtypeStruct(router_t.shape, F32)),
        in_specs=[anywhere] * 4 + [vmem] * 3,
        out_specs=(anywhere,) * 4 + (vmem,),
        scratch_shapes=[
            pltpu.VMEM((3, *gate.shape), BF16),
            pltpu.VMEM(direct.shape, BF16),
            pltpu.SemaphoreType.DMA((4, 4)),
            pltpu.SemaphoreType.DMA((4, 4)),
        ],
        compiler_params=pltpu.CompilerParams(vmem_limit_bytes=60 * 2**20),
        name="finish",
    )(gate, up, down, direct, source, means, router_t)


def shards(activations, cotangent, router, gate_experts, up_experts, down_experts, route_source):
    router_t = router.T
    gate_t, up_t, down_t, source, means, direct = moved(
        activations, cotangent, gate_experts.transpose(0, 2, 1), up_experts.transpose(0, 2, 1),
        down_experts, router_t, route_source,
    )
    gate_t, up_t, down_t, input_grad, router_grad = finish(
        gate_t, up_t, down_t, direct, source, means, router_t
    )
    return (
        input_grad, gate_t.transpose(0, 2, 1), up_t.transpose(0, 2, 1), down_t, router_grad.T,
    )


def solution(mesh):
    in_specs = (
        P("row", None),
        P("row", None),
        P(),
        P(None, "row", "col"),
        P(None, "row", "col"),
        P(None, "col", "row"),
        P(),
    )
    out_specs = (
        P("row", None),
        P(None, "row", "col"),
        P(None, "row", "col"),
        P(None, "col", "row"),
        P(),
    )
    return jax.shard_map(shards, mesh=mesh, in_specs=in_specs, out_specs=out_specs, check_vma=False)
```

```python
import functools

import jax
import jax.numpy as jnp
from jax import lax
from jax.experimental import pallas as pl
from jax.experimental.pallas import tpu as pltpu
from jax.sharding import PartitionSpec as P

SEG = 256
EXPERTS = 16
SIDE = 4
DEPTH = 8
BLOCK = 128
HALF = 176
LANES = 3 * BLOCK
WIDE = SIDE * BLOCK
GROUP = 16
CHUNK = 16
PIECE = 32
PRECISE = lax.Precision.HIGHEST
MESH = pl.DeviceIdType.MESH
F32 = jnp.float32
BF16 = jnp.bfloat16


def dot_nn(a, b):
    return lax.dot_general(a, b, (((1,), (0,)), ((), ())), preferred_element_type=F32)


def dot_nt(a, b):
    return lax.dot_general(a, b, (((1,), (1,)), ((), ())), preferred_element_type=F32)


def dot_tn(a, b):
    return lax.dot_general(a, b, (((0,), (0,)), ((), ())), preferred_element_type=F32)


def drain(ref, sem):
    pltpu.make_async_copy(ref, ref, sem).wait()


def kernel(
    act, cot, gate_t, up_t, down, router_t, wanted,
    gate_out, up_out, down_out, source_out, means_out, direct_out,
    experts, tokens, merged, weights, terms, part_out, part_mid, part_in, deltas,
    direct, from_pair, to_depth, from_depth, depth_sum, to_owner, direct_all, inner,
    spread, spread_t, scores, means, routes, in_row, in_col, source, chooser,
    e_sem, tok_sem, tok_send, near_sem, near_send, pass_sem, pass_send, m_send, m_recv, p_send, mid_recv, p_recv, d_send, d_recv, d_pass,
    t_send, t_recv, s_send, s_recv, z_send, z_recv, z_pass, o_send, o_recv, a_send, a_recv, a_pass,
    f_send, f_recv, out_sem, c_send, c_recv, n_send, n_recv, r_send, r_recv, l_send, l_recv,
):
    row = lax.axis_index("row")
    col = lax.axis_index("col")
    x, y = row // SIDE, row % SIDE
    z, k = col // 2, col % 2
    sibling = (row, z * 2 + 1 - k)

    def line(h, at):
        return jnp.where(h == 0, at * SIDE + y, x * SIDE + at)

    def cross(h, at):
        return jnp.where(h == 0, x * SIDE + at, at * SIDE + y)

    def nth(t):
        return jnp.where(t == 0, 2, jnp.where(t == 1, 1, jnp.where(t == 2, 3, 0)))

    def send(src, dst, send_sem, recv_sem, to):
        pltpu.make_async_remote_copy(
            src_ref=src, dst_ref=dst, send_sem=send_sem, recv_sem=recv_sem,
            device_id=to, device_id_type=MESH,
        ).start()

    loads = [
        pltpu.make_async_copy(src, experts.at[:, :, pl.ds(n * BLOCK, BLOCK)], e_sem.at[n])
        for n, src in enumerate((gate_t, up_t, down))
    ]
    read = pltpu.make_async_copy(act, direct_all, out_sem.at[0, 0])
    read.start()
    for load in loads:
        load.start()

    rows_all = SIDE * SIDE
    cols_all = 2 * DEPTH
    barrier = pltpu.get_barrier_semaphore()

    @pl.loop(1, rows_all)
    def _(o):
        pl.semaphore_signal(
            barrier, inc=1, device_id=((row + o) % rows_all, col), device_id_type=MESH
        )

    @pl.loop(1, cols_all)
    def _(o):
        pl.semaphore_signal(
            barrier, inc=1, device_id=(row, (col + o) % cols_all), device_id_type=MESH
        )

    read.wait()
    found = []
    for b in range(2):
        def add(i, total):
            at = pl.multiple_of(b * SEG + i * GROUP, GROUP)
            return total + direct_all[pl.ds(at, GROUP), :].astype(F32)

        total = lax.fori_loop(0, SEG // GROUP, add, jnp.zeros((GROUP, 4 * WIDE), F32))
        found.append(jnp.sum(total, axis=0, keepdims=True) / SEG)
        for q in range(rows_all):
            means[row, b * rows_all + q:b * rows_all + q + 1, :] = found[b][:, q * BLOCK:(q + 1) * BLOCK]
    found.append(jnp.zeros((6, 4 * WIDE), F32))
    scores[row] = jnp.zeros((8, BLOCK), F32)
    scores[row, :, 0:EXPERTS] = lax.dot_general(
        jnp.concatenate(found, axis=0), router_t[...], (((1,), (1,)), ((), ())),
        precision=PRECISE, preferred_element_type=F32,
    )
    pl.semaphore_wait(barrier, rows_all + cols_all - 2)

    @pl.loop(1, rows_all)
    def _(o):
        send(scores.at[row], scores.at[row], c_send, c_recv, ((row + o) % rows_all, col))

    first = pl.multiple_of((k * SIDE + z % SIDE) * PIECE, PIECE)
    piece = pl.ds(first, PIECE)

    @pl.loop(0, 2)
    def _(b):
        rows = pl.ds(pl.multiple_of(b * SEG + first, PIECE), PIECE)
        for o in range(1, SIDE):
            for n, src in enumerate((act, cot)):
                to = (x + o) % SIDE
                j = SIDE * b + x
                send(
                    src.at[rows, pl.ds(pl.multiple_of(to * WIDE, WIDE), WIDE)],
                    tokens.at[0, j, n, piece], tok_send, tok_sem.at[0, j], (to * SIDE + y, col),
                )
                to = (y + o) % SIDE
                j = SIDE * b + y
                for q in range(SIDE):
                    send(
                        src.at[rows, pl.ds(pl.multiple_of((q * SIDE + to) * BLOCK, BLOCK), BLOCK)],
                        tokens.at[1, j, n, piece, pl.ds(q * BLOCK, BLOCK)],
                        tok_send, tok_sem.at[1, j], (x * SIDE + to, col),
                    )

    for b in range(2):
        rows = pl.ds(b * SEG, SEG)
        for n, src in enumerate((act, cot)):
            pltpu.make_async_copy(
                src.at[rows, pl.ds(pl.multiple_of(x * WIDE, WIDE), WIDE)],
                tokens.at[0, SIDE * b + x, n], tok_sem.at[0, SIDE * b + x],
            ).start()
            for q in range(SIDE):
                pltpu.make_async_copy(
                    src.at[rows, pl.ds(pl.multiple_of((q * SIDE + y) * BLOCK, BLOCK), BLOCK)],
                    tokens.at[1, SIDE * b + y, n, :, pl.ds(q * BLOCK, BLOCK)],
                    tok_sem.at[1, SIDE * b + y],
                ).start()
    for s in range(2 * rows_all):
        at = (s % 2) * rows_all + s // 2
        v = wanted[s]
        place = (v // 2) * 8 + v % 2
        lanes = lax.broadcasted_iota(jnp.int32, (1, BLOCK), 1)
        chooser[at:at + 1, :] = jnp.where(lanes == place, 1.0, 0.0).astype(F32)

    drain(scores.at[0:rows_all - 1], c_recv)
    logits = lax.dot_general(
        chooser[...], scores[...].reshape(rows_all * 8, BLOCK), (((1,), (0,)), ((), ())),
        precision=PRECISE, preferred_element_type=F32,
    )
    real = lax.broadcasted_iota(jnp.int32, logits.shape, 1) < EXPERTS
    powers = jnp.where(real, jnp.exp(logits), 0.0)
    routes[...] = powers / jnp.sum(powers, axis=1, keepdims=True)
    span = EXPERTS * GROUP

    def iota(shape, axis):
        return lax.broadcasted_iota(jnp.int32, shape, axis)

    same = iota((span, span), 0) % GROUP == iota((span, span), 1) % GROUP
    pick = (iota((span, rows_all), 0) // GROUP == iota((span, rows_all), 1)).astype(BF16)
    expand = (iota((span, BLOCK), 0) // GROUP == iota((span, BLOCK), 1)).astype(BF16)
    for b in range(2):
        rounded = routes[b * rows_all:(b + 1) * rows_all, :].astype(BF16)
        long = dot_nt(dot_nn(pick, rounded).astype(BF16), expand)
        spread[b] = jnp.where(same, long, 0.0).astype(BF16)
        long = dot_nt(dot_nt(expand, rounded).astype(BF16), pick)
        spread_t[b] = jnp.where(same, long, 0.0).astype(BF16)

    def others(b, h):
        own = x if h == 0 else y
        return [SIDE * b + (own + o) % SIDE for o in range(1, SIDE)]

    def pass_tokens(b):
        for o in range(SIDE - 1):
            for h in range(2):
                j = others(b, h)[o]
                drain(tokens.at[0, 0, :, 0:PIECE], tok_sem.at[h, j])
                both = tokens.at[h, j, :, piece]
                for step in (1, DEPTH - 1):
                    to = (row, (z + step) % DEPTH * 2 + k)
                    send(both, both, near_send.at[0], near_sem.at[h, j], to)
                for n, step in enumerate((2, DEPTH - 2)):
                    one = tokens.at[h, j, n, piece]
                    to = (row, (z + step) % DEPTH * 2 + k)
                    send(one, one, near_send.at[1], near_sem.at[h, j], to)

    for load in loads:
        load.wait()

    for b in range(2):
        if b == 1:
            pass_tokens(0)
            pass_tokens(1)
        for h in range(2):

            @pl.loop(0, HALF // GROUP)
            def _(g):
                at = pl.multiple_of(g * GROUP, GROUP)
                chunk = experts[:, pl.ds(h * HALF + at, GROUP), :].reshape(EXPERTS * GROUP, LANES)
                out = dot_nn(spread[b], chunk).astype(BF16)
                merged[h, b, :, pl.ds(at, GROUP), :] = out.reshape(SIDE * SIDE, GROUP, LANES)

            own = x if h == 0 else y
            side = y if h == 0 else x

            @pl.loop(0, SIDE)
            def _(t):
                q = (own + nth(t)) % SIDE
                for o in range(SIDE):
                    to = (side + o) % SIDE
                    slot = q * SIDE + to if h == 0 else to * SIDE + q
                    src = merged.at[h, b, slot]
                    dst = weights.at[h, SIDE * b + q, side]
                    if o == 0:
                        pltpu.make_async_copy(src, dst, m_recv.at[h, SIDE * b + q]).start()
                    else:
                        device = x * SIDE + to if h == 0 else to * SIDE + y
                        send(src, dst, m_send.at[h, b], m_recv.at[h, SIDE * b + q], (device, col))

    def joined(h, j, n):
        return jnp.concatenate(
            [weights[h, j, q, :, n * BLOCK:(n + 1) * BLOCK] for q in range(SIDE)], axis=1
        )

    def forward(b):
        own_half = pl.ds(pl.multiple_of(k * (SEG // 2), SEG // 2), SEG // 2)
        for o in range(SIDE - 1):
            for h in range(2):
                j = others(b, h)[o]
                drain(tokens.at[0, 0, :, 0:3 * PIECE], near_sem.at[h, j])
                part = tokens.at[h, j, :, own_half]
                send(part, part, pass_send.at[b], pass_sem.at[h, j], sibling)

        @pl.loop(0, 8)
        def _(i):
            t, h = i // 2, i % 2
            own = jnp.where(h == 0, x, y)
            q = (own + nth(t)) % SIDE
            j = SIDE * b + q
            drain(weights.at[h, j], m_recv.at[h, j])

            @pl.when(t < SIDE - 1)
            def _():
                drain(tokens.at[0, 0, :, 0:SEG // 2], pass_sem.at[h, j])

            @pl.when(t == SIDE - 1)
            def _():
                drain(tokens.at[h, j], tok_sem.at[h, j])

            for n in range(3):
                side = tokens[h, j, 0 if n < 2 else 1]
                part_out[h, j, n] = dot_nt(joined(h, j, n), side).astype(BF16)

            @pl.when(t == 0)
            def _():
                for n, o in enumerate((SIDE - 1, 1)):
                    send(
                        part_out.at[h, j, :, :, pl.ds(n * BLOCK, BLOCK)], part_mid.at[h, b, n],
                        p_send.at[h, j], mid_recv.at[h, b, n], (line(h, (own + o) % SIDE), col),
                    )

    forward(0)
    forward(1)

    @pl.loop(0, 4)
    def _(i):
        b, h = i // 2, i % 2
        own = jnp.where(h == 0, x, y)
        for t, o in enumerate((1, SIDE - 1)):
            n = 1 - t
            q = (own + o) % SIDE
            j = SIDE * b + q
            lanes = slice(n * BLOCK, (n + 1) * BLOCK)
            drain(part_mid.at[h, b, n], mid_recv.at[h, b, n])
            for m in range(3):
                both = part_out[h, j, m, :, lanes].astype(F32) + part_mid[h, b, n, m].astype(F32)
                part_out[h, j, m, :, lanes] = both.astype(BF16)
            send(part_out.at[h, j], part_in.at[h, b, t], p_send.at[h, j], p_recv.at[h, b], (line(h, q), col))

    @pl.loop(0, 4)
    def _(i):
        b, h = i // 2, i % 2
        own = jnp.where(h == 0, x, y)
        j = SIDE * b + own
        drain(part_in.at[h, b], p_recv.at[h, b])

        def total(n):
            out = part_out[h, j, n].astype(F32)
            for o in range(2):
                out += part_in[h, b, o, n].astype(F32)
            return out

        gate, up, grad = total(0), total(1), total(2)
        sig = jax.nn.sigmoid(gate)
        gated = gate * sig
        deltas[h, j, 0] = (grad * up * sig * (1.0 + gate * (1.0 - sig))).astype(BF16)
        deltas[h, j, 1] = (grad * gated).astype(BF16)
        deltas[h, j, 2] = (gated * up).astype(BF16)
        for o in (1, SIDE - 1):
            send(
                deltas.at[h, j], deltas.at[h, j], d_send.at[h, b], d_recv.at[h, j],
                (line(h, (own + o) % SIDE), col),
            )

    @pl.loop(0, 4)
    def _(i):
        b, h = i // 2, i % 2
        own = jnp.where(h == 0, x, y)
        for n, o in ((1, 1), (0, SIDE - 1)):
            j = SIDE * b + (own + o) % SIDE
            drain(deltas.at[h, j], d_recv.at[h, j])
            part = deltas.at[h, j, :, :, pl.ds(n * BLOCK, BLOCK)]
            send(part, part, d_pass.at[h, b], d_recv.at[h, j], (line(h, (own - o + SIDE) % SIDE), col))

    def item(i):
        b, t, h = i // 8, (i // 2) % SIDE, i % 2
        own = jnp.where(h == 0, x, y)
        q = (own + jnp.where(t < 2, t, 5 - t)) % SIDE
        return b, t, h, q, SIDE * b + q

    def above(o):
        return (row, (z + o) % DEPTH * 2 + k)

    def pair_sum(i):
        b, t, h, q, j = item(i)
        drain(from_pair.at[h, j], s_recv.at[h, j])
        out = direct[i % 4, k].astype(F32) + from_pair[h, j].astype(F32)
        to_depth[h, j] = out.astype(BF16).reshape(DEPTH, CHUNK, WIDE)

        def hop(target, over, slot, sem):
            to = (z + target) % DEPTH
            send(to_depth.at[h, j, to], from_depth.at[h, j, slot], z_send.at[h, j], sem.at[h, j], above(over))

        hop(DEPTH - 3, DEPTH - 1, 4, z_pass)
        hop(3, 1, 5, z_pass)
        hop(4, DEPTH - 2, 6, z_pass)
        hop(1, 1, 0, z_recv)
        hop(DEPTH - 1, DEPTH - 1, 1, z_recv)

    def pass_sum(i):
        b, t, h, q, j = item(i)
        drain(from_depth.at[h, j, 4:7], z_pass.at[h, j])
        for o, slots, into in ((DEPTH - 2, (4, 6), 2), (2, (5,), 3)):
            to = (z + o) % DEPTH
            out = to_depth[h, j, to].astype(F32)
            for slot in slots:
                out += from_depth[h, j, slot].astype(F32)
            to_depth[h, j, to] = out.astype(BF16)
            send(to_depth.at[h, j, to], from_depth.at[h, j, into], z_send.at[h, j], z_recv.at[h, j], above(o))

    def send_terms(i):
        b, t, h, q, j = item(i)
        side = jnp.where(h == 0, y, x)
        slot = jnp.where(h == 0, q * SIDE + y, x * SIDE + q)
        for o in range(1, SIDE):
            to = (side + o) % SIDE
            send(
                weights.at[h, j, to], terms.at[h, b, slot], t_send.at[h, j], t_recv.at[h, b],
                (cross(h, to), col),
            )
        pltpu.make_async_copy(weights.at[h, j, side], terms.at[h, b, slot], t_recv.at[h, b]).start()

    def backward(i):
        b, t, h, q, j = item(i)

        @pl.when(t == SIDE - 1)
        def _():
            drain(deltas.at[h, j], d_recv.at[h, j])

        @pl.when(i >= 4)
        def _():
            drain(direct.at[0, 0], s_send.at[i % 4])

        both = deltas[h, j, 0:2].reshape(2 * HALF, SEG)
        out = dot_tn(both, jnp.concatenate([joined(h, j, 0), joined(h, j, 1)], axis=0))
        direct[i % 4] = out.astype(BF16).reshape(2, SEG // 2, WIDE)
        send(direct.at[i % 4, 1 - k], from_pair.at[h, j], s_send.at[i % 4], s_recv.at[h, j], sibling)

        for n in range(3):
            side = tokens[h, j, 0 if n < 2 else 1]
            out = dot_nn(deltas[h, j, n], side).astype(BF16)
            for p in range(SIDE):
                weights[h, j, p, :, n * BLOCK:(n + 1) * BLOCK] = out[:, p * BLOCK:(p + 1) * BLOCK]

        @pl.when(i > 0)
        def _():
            pair_sum(i - 1)

        @pl.when(i > 1)
        def _():
            pass_sum(i - 2)

    def depth_sums(b):
        @pl.loop(0, 8)
        def _(i):
            _, t, h, q, j = item(b * 8 + i)
            drain(from_depth.at[h, j, 0:4], z_recv.at[h, j])
            out = to_depth[h, j, z].astype(F32)
            for o in range(4):
                out += from_depth[h, j, o].astype(F32)
            depth_sum[h, j] = out.astype(BF16)
            own = jnp.where(h == 0, x, y)

            @pl.when(t == 0)
            def _():
                to_owner[h, b, own] = out.astype(BF16)

            @pl.when(t > 0)
            def _():
                send(
                    depth_sum.at[h, j], to_owner.at[h, b, own], o_send.at[h, b], o_recv.at[h, b],
                    (line(h, q), col),
                )

    def place(b, o=0):
        at = b * SEG + k * (SEG // 2) + (z + o) % DEPTH * CHUNK
        return direct_all.at[pl.ds(pl.multiple_of(at, CHUNK), CHUNK)]

    def half(b):
        return pl.ds(pl.multiple_of(b * SEG + k * (SEG // 2), SEG // 2), SEG // 2)

    def spread_direct(b):
        for h in range(2):
            drain(to_owner.at[h, b, 0:3], o_recv.at[h, b])
        pieces = []
        for p in range(SIDE):
            for q in range(SIDE):
                one = to_owner[0, b, p, :, q * BLOCK:(q + 1) * BLOCK].astype(F32)
                two = to_owner[1, b, q, :, p * BLOCK:(p + 1) * BLOCK].astype(F32)
                pieces.append((one + two).astype(BF16))
        place(b)[...] = jnp.concatenate(pieces, axis=1)
        for o in (1, DEPTH - 1):
            send(place(b), place(b), a_send.at[b], a_recv.at[b], above(o))
        for n, o in enumerate((2, DEPTH - 2)):
            send(place(b), place(b), a_send.at[b], a_pass.at[b, n], above(o))

    def pass_direct(b):
        for n, (back, steps) in enumerate(((DEPTH - 2, (1, 2)), (2, (DEPTH - 1,)))):
            drain(place(b, back), a_pass.at[b, n])
            for o in steps:
                send(place(b, back), place(b, back), a_send.at[b], a_recv.at[b], above(o))

    def share_direct(b):
        drain(direct_all.at[0:5 * CHUNK], a_recv.at[b])
        send(direct_all.at[half(b)], direct_all.at[half(b)], f_send.at[b], f_recv.at[b], sibling)

    def group(h, g):
        at = pl.multiple_of(g * GROUP, GROUP)
        return at, experts[:, pl.ds(h * HALF + at, GROUP), :].reshape(span, LANES)

    def products(b):
        inner[b] = jnp.zeros((span, span), F32)
        for h in range(2):
            drain(terms.at[h, b], t_recv.at[h, b])

            @pl.loop(0, HALF // GROUP, unroll=True)
            def _(g):
                at, chunk = group(h, g)
                term = terms[h, b, :, pl.ds(at, GROUP), :].reshape(span, LANES)
                inner[b] += dot_nt(term, chunk)

    def gradients(h):
        for b in range(2):
            drain(merged.at[h, b, 0:12], m_send.at[h, b])

        @pl.loop(0, HALF // GROUP, unroll=True)
        def _(g):
            at = pl.multiple_of(g * GROUP, GROUP)
            out = None
            for b in range(2):
                term = terms[h, b, :, pl.ds(at, GROUP), :].reshape(span, LANES)
                part = dot_nn(spread_t[b], term)
                out = part if out is None else out + part
            merged[h, 0, :, pl.ds(at, GROUP), :] = out.astype(BF16).reshape(EXPERTS, GROUP, LANES)

        for n, dst in enumerate((gate_out, up_out, down_out)):
            pltpu.make_async_copy(
                merged.at[h, 0, :, :, pl.ds(n * BLOCK, BLOCK)],
                dst.at[:, pl.ds(h * HALF, HALF), :], out_sem.at[h, n],
            ).start()

    @pl.loop(0, 12)
    def _(i):
        backward(i)
        send_terms(i)

    depth_sums(0)

    @pl.loop(12, 16)
    def _(i):
        backward(i)
        send_terms(i)

    pair_sum(15)
    pass_sum(14)
    pass_sum(15)
    spread_direct(0)
    depth_sums(1)
    products(0)
    pass_direct(0)
    spread_direct(1)
    products(1)

    fold = (iota((span, BLOCK), 0) // GROUP == iota((span, BLOCK), 1) % EXPERTS).astype(F32)
    here = iota((rows_all, BLOCK), 1) // EXPERTS == iota((rows_all, BLOCK), 0) % 8
    packed = []
    for b in range(2):
        kept = jnp.sum(jnp.where(same, inner[b], 0.0).reshape(EXPERTS, GROUP, span), axis=1)
        dense = lax.dot_general(
            kept, fold, (((1,), (0,)), ((), ())), precision=PRECISE, preferred_element_type=F32
        )
        packed.append(jnp.sum(jnp.where(here, dense, 0.0).reshape(2, 8, BLOCK), axis=1))
    packed.append(jnp.zeros((4, BLOCK), F32))
    in_row[0] = jnp.concatenate(packed, axis=0)

    @pl.loop(1, rows_all)
    def _(o):
        send(in_row.at[0], in_row.at[o], r_send, r_recv, ((row + o) % rows_all, col))

    pass_direct(1)
    share_direct(0)
    gradients(0)
    drain(in_row.at[1:rows_all], r_recv)

    @pl.loop(1, rows_all)
    def _(o):
        send(means.at[row], means.at[row], n_send, n_recv, ((row + o) % rows_all, col))

    out = in_row[0]
    for o in range(1, rows_all):
        out += in_row[o]
    in_col[0] = out

    @pl.loop(1, cols_all)
    def _(o):
        send(in_col.at[0], in_col.at[o], l_send, l_recv, (row, (col + o) % cols_all))

    gradients(1)
    share_direct(1)
    for b in range(2):
        drain(direct_all.at[0:SEG // 2], f_recv.at[b])
    copy = pltpu.make_async_copy(direct_all, direct_out, e_sem.at[0])
    copy.start()
    drain(in_col.at[1:cols_all], l_recv)
    out = in_col[0]
    for o in range(1, cols_all):
        out += in_col[o]
    wide = jnp.concatenate(
        [jnp.broadcast_to(out[p:p + 1, :], (8, BLOCK)) for p in range(4)], axis=0
    )
    shape = (2 * rows_all, BLOCK)
    wide = jnp.where(iota(shape, 1) // EXPERTS == iota(shape, 0) % 8, wide, 0.0)
    narrow = (iota((BLOCK, BLOCK), 0) % EXPERTS == iota((BLOCK, BLOCK), 1)).astype(F32)
    total = lax.dot_general(
        wide, narrow, (((1,), (0,)), ((), ())), precision=PRECISE, preferred_element_type=F32
    )
    logit_grad = routes[...] * (total - jnp.sum(routes[...] * total, axis=1, keepdims=True))
    source[...] = lax.dot_general(
        chooser[...], logit_grad, (((0,), (0,)), ((), ())),
        precision=PRECISE, preferred_element_type=F32,
    ).reshape(rows_all, 8, BLOCK)
    source_out[...] = source[...]
    drain(means.at[0:rows_all - 1], n_recv)
    means_out[...] = means[...]

    for h in range(2):
        for b in range(2):
            drain(deltas.at[h, 0:2], d_send.at[h, b])
            drain(deltas.at[h, 0], d_pass.at[h, b])
            drain(depth_sum.at[h, 0:3], o_send.at[h, b])
        own = x if h == 0 else y

        @pl.loop(0, 8)
        def _(j):
            @pl.when(j % SIDE != own)
            def _():
                drain(part_out.at[h, 0], p_send.at[h, j])

            drain(weights.at[h, 0, 0:3], t_send.at[h, j])
            drain(to_depth.at[h, 0, 0:7], z_send.at[h, j])

        for n in range(3):
            drain(merged.at[h, 0, :, :, pl.ds(n * BLOCK, BLOCK)], out_sem.at[h, n])
    for n in range(4):
        drain(direct.at[0, 0], s_send.at[n])
    drain(tokens.at[0, 0:3, 0], tok_send)
    drain(tokens.at[0, 0:3], near_send.at[0])
    drain(tokens.at[0, 0:3, 0], near_send.at[1])
    for b in range(2):
        drain(tokens.at[0, 0:3], pass_send.at[b])
        drain(direct_all.at[0:7 * CHUNK], a_send.at[b])
        drain(direct_all.at[0:SEG // 2], f_send.at[b])
    drain(scores.at[0:rows_all - 1], c_send)
    drain(means.at[0:rows_all - 1], n_send)
    drain(in_row.at[1:rows_all], r_send)
    drain(in_col.at[1:cols_all], l_send)
    copy.wait()


def moved(act, cot, gate_t, up_t, down, router_t, wanted):
    units = gate_t.shape[1]
    grad = jax.ShapeDtypeStruct((EXPERTS, units, BLOCK), BF16)
    vmem = pl.BlockSpec(memory_space=pltpu.VMEM)
    anywhere = pl.BlockSpec(memory_space=pl.ANY)
    dma = pltpu.SemaphoreType.DMA
    segs = SIDE * SIDE
    return pl.pallas_call(
        kernel,
        out_shape=(
            grad, grad, grad,
            jax.ShapeDtypeStruct((segs, 8, BLOCK), F32),
            jax.ShapeDtypeStruct((segs, 2 * segs, BLOCK), F32),
            jax.ShapeDtypeStruct((2 * SEG, 4 * WIDE), BF16),
        ),
        in_specs=[anywhere] * 5 + [vmem, pl.BlockSpec(memory_space=pltpu.SMEM)],
        out_specs=(anywhere, anywhere, anywhere, vmem, vmem, anywhere),
        scratch_shapes=[
            pltpu.VMEM((EXPERTS, 2 * HALF, LANES), BF16),
            pltpu.VMEM((2, 8, 2, SEG, WIDE), BF16),
            pltpu.VMEM((2, 2, segs, HALF, LANES), BF16),
            pltpu.VMEM((2, 8, SIDE, HALF, LANES), BF16),
            pltpu.VMEM((2, 2, segs, HALF, LANES), BF16),
            pltpu.VMEM((2, 8, 3, HALF, SEG), BF16),
            pltpu.VMEM((2, 2, 2, 3, HALF, BLOCK), BF16),
            pltpu.VMEM((2, 2, 2, 3, HALF, SEG), BF16),
            pltpu.VMEM((2, 8, 3, HALF, SEG), BF16),
            pltpu.VMEM((4, 2, SEG // 2, WIDE), BF16),
            pltpu.VMEM((2, 8, SEG // 2, WIDE), BF16),
            pltpu.VMEM((2, 8, DEPTH, CHUNK, WIDE), BF16),
            pltpu.VMEM((2, 8, DEPTH - 1, CHUNK, WIDE), BF16),
            pltpu.VMEM((2, 8, CHUNK, WIDE), BF16),
            pltpu.VMEM((2, 2, SIDE, CHUNK, WIDE), BF16),
            pltpu.VMEM((2 * SEG, 4 * WIDE), BF16),
            pltpu.VMEM((2, EXPERTS * GROUP, EXPERTS * GROUP), F32),
            pltpu.VMEM((2, EXPERTS * GROUP, EXPERTS * GROUP), BF16),
            pltpu.VMEM((2, EXPERTS * GROUP, EXPERTS * GROUP), BF16),
            pltpu.VMEM((segs, 8, BLOCK), F32),
            pltpu.VMEM((segs, 2 * segs, BLOCK), F32),
            pltpu.VMEM((2 * segs, BLOCK), F32),
            pltpu.VMEM((segs, 8, BLOCK), F32),
            pltpu.VMEM((2 * DEPTH, 8, BLOCK), F32),
            pltpu.VMEM((segs, 8, BLOCK), F32),
            pltpu.VMEM((2 * segs, BLOCK), F32),
            dma((3,)), dma((2, 8)), dma, dma((2, 8)), dma((2,)), dma((2, 8)), dma((2,)),
            dma((2, 2)), dma((2, 8)), dma((2, 8)), dma((2, 2, 2)), dma((2, 2)), dma((2, 2)), dma((2, 8)), dma((2, 2)),
            dma((2, 8)), dma((2, 2)), dma((4,)), dma((2, 8)), dma((2, 8)), dma((2, 8)), dma((2, 8)),
            dma((2, 2)), dma((2, 2)), dma((2,)), dma((2,)), dma((2, 2)), dma((2,)), dma((2,)), dma((2, 3)),
            dma, dma, dma, dma, dma, dma, dma, dma,
        ],
        compiler_params=pltpu.CompilerParams(
            collective_id=1, has_side_effects=True, vmem_limit_bytes=63 * 2**20
        ),
        cost_estimate=pl.CostEstimate(flops=12 * 10**9, bytes_accessed=16 * 10**6, transcendentals=0),
        name="experts",
    )(act, cot, gate_t, up_t, down, router_t, wanted)


def finish_kernel(
    gate, up, down, direct, source, means, router_t,
    gate_out, up_out, down_out, input_out, router_out, grads, rows, in_sem, out_sem,
):
    parts = in_sem.shape[1]
    pairs = ((gate, gate_out), (up, up_out), (down, down_out))

    def pieces(n, p, size):
        at = pl.ds(p * (size // parts), size // parts)
        if n == 3:
            return direct.at[at], rows.at[at], input_out.at[at]
        return pairs[n][0].at[at], grads.at[n, at], pairs[n][1].at[at]

    sizes = [EXPERTS] * 3 + [rows.shape[0]]
    order = [(n, p) for p in range(parts) for n in (3, 0, 1, 2)]
    for n, p in order:
        src, mid, _ = pieces(n, p, sizes[n])
        pltpu.make_async_copy(src, mid, in_sem.at[n, p]).start()
    own = source[lax.axis_index("row")]
    mean_grad = lax.dot_general(
        own[:, 0:EXPERTS], router_t[...], (((1,), (0,)), ((), ())),
        precision=PRECISE, preferred_element_type=F32,
    ) / SEG
    for n, p in order:
        src, mid, dst = pieces(n, p, sizes[n])
        pltpu.make_async_copy(src, mid, in_sem.at[n, p]).wait()
        if n == 3:
            size = sizes[n] // parts
            extra = mean_grad[p * size // SEG:p * size // SEG + 1, :]

            @pl.loop(0, size // GROUP)
            def _(i):
                at = pl.ds(pl.multiple_of(p * size + i * GROUP, GROUP), GROUP)
                rows[at, :] = (rows[at, :].astype(F32) + extra).astype(BF16)

        pltpu.make_async_copy(mid, dst, out_sem.at[n, p]).start()
    segs = means.shape[0]
    out = None
    for b in range(2):
        rows_b = jnp.concatenate([means[:, b * segs + q, :] for q in range(segs)], axis=1)
        part = lax.dot_general(
            source[:, b, 0:EXPERTS], rows_b, (((0,), (0,)), ((), ())),
            precision=PRECISE, preferred_element_type=F32,
        )
        out = part if out is None else out + part
    router_out[...] = out
    for n, p in order:
        _, mid, dst = pieces(n, p, sizes[n])
        pltpu.make_async_copy(mid, dst, out_sem.at[n, p]).wait()


def finish(gate, up, down, direct, source, means, router_t):
    vmem = pl.BlockSpec(memory_space=pltpu.VMEM)
    anywhere = pl.BlockSpec(memory_space=pl.ANY)
    like = [jax.ShapeDtypeStruct(v.shape, v.dtype) for v in (gate, up, down, direct)]
    return pl.pallas_call(
        finish_kernel,
        out_shape=(*like, jax.ShapeDtypeStruct(router_t.shape, F32)),
        in_specs=[anywhere] * 4 + [vmem] * 3,
        out_specs=(anywhere,) * 4 + (vmem,),
        scratch_shapes=[
            pltpu.VMEM((3, *gate.shape), BF16),
            pltpu.VMEM(direct.shape, BF16),
            pltpu.SemaphoreType.DMA((4, 4)),
            pltpu.SemaphoreType.DMA((4, 4)),
        ],
        compiler_params=pltpu.CompilerParams(vmem_limit_bytes=60 * 2**20),
        name="finish",
    )(gate, up, down, direct, source, means, router_t)


def shards(activations, cotangent, router, gate_experts, up_experts, down_experts, route_source):
    router_t = router.T
    gate_t, up_t, down_t, source, means, direct = moved(
        activations, cotangent, gate_experts.transpose(0, 2, 1), up_experts.transpose(0, 2, 1),
        down_experts, router_t, route_source,
    )
    gate_t, up_t, down_t, input_grad, router_grad = finish(
        gate_t, up_t, down_t, direct, source, means, router_t
    )
    return (
        input_grad, gate_t.transpose(0, 2, 1), up_t.transpose(0, 2, 1), down_t, router_grad.T,
    )


def solution(mesh):
    in_specs = (
        P("row", None),
        P("row", None),
        P(),
        P(None, "row", "col"),
        P(None, "row", "col"),
        P(None, "col", "row"),
        P(),
    )
    out_specs = (
        P("row", None),
        P(None, "row", "col"),
        P(None, "row", "col"),
        P(None, "col", "row"),
        P(),
    )
    return jax.shard_map(shards, mesh=mesh, in_specs=in_specs, out_specs=out_specs, check_vma=False)
```
